128 devices in a mesh: ctx: 32 (over x, y_lo, z), tp: 4 (over y_hi, core).
Axes of the slice: x: 4, y: 4 (y_hi: 2, y_lo: 2; y = y_hi * 2 + y_lo), z: 4, core: 2. Of those that a mesh axis runs over, the one named last changes fastest.
Arguments:
- mixer_input: bfloat16 [8192, 4096], P('ctx', 'tp'), may hold values from -6 to 6
- gate_in: bfloat16 [8192, 4096], P('ctx', 'tp'), may hold values from -6 to 6
- gate_out: bfloat16 [8192, 4096], P('ctx', 'tp'), may hold values from -18 to 18
- residue: float32 [4096, 16], P('tp'), may hold values from -26 to 26
- decay_rate: float32 [4096, 16], P('tp'), may hold values from 3.0517578e-05 to 0.04
- norm_gain: float32 [4096], P('tp'), may hold values from 0.1 to 1.9
- queries: bfloat16 [8192, 4096], P('ctx', 'tp'), may hold values from -10 to 10
- key_vectors: bfloat16 [8192, 4096], P('ctx', 'tp'), may hold values from -10 to 10
- grad_out: bfloat16 [8192, 4096], P('ctx', 'tp'), may hold values from -6 to 6
Outputs:
- attended: bfloat16 [8192, 4096], P('ctx', 'tp')
- grad_queries: bfloat16 [8192, 4096], P('ctx', 'tp')
- grad_keys: bfloat16 [8192, 4096], P('ctx', 'tp')
- grad_input: bfloat16 [8192, 4096], P('ctx', 'tp')
The draws below stay inside these ranges and needn't reach their ends.
All inputs are finite; a program needn't handle non-finite values.
Results may differ from the reference program's by a relative error of at most 0.025.
Values may be sent and summed in bfloat16 or wider, within the bound.
No kernel may reach another device: no remote copies, remote signals or barrier semaphores. Data moves between devices by JAX's collectives and lax.ppermute only.
A program may use at most 192 MiB of HBM per device.

```python
import math
import jax
import jax.numpy as jnp
from jax import lax

HEADS = 32
HEAD_DIM = 128
MODES = 16
SPAN = 2
TOK_DEV = 256
LENGTH = 8192
WIDTH = 4096
N_CTX = 32


def draw_queries(key, part):
    own = jax.random.fold_in(key, 11)
    return jnp.clip(jax.random.normal(own, (LENGTH, WIDTH), jnp.float32), -6.0, 6.0).astype(jnp.bfloat16)


def draw_key_vectors(key, part):
    own = jax.random.fold_in(key, 17)
    return jnp.clip(jax.random.normal(own, (LENGTH, WIDTH), jnp.float32), -6.0, 6.0).astype(jnp.bfloat16)


def draw_decay_rate(key, part):
    key = jax.random.fold_in(key, 23)
    pick_key, slow_key, fast_key, broad_key = jax.random.split(key, 4)
    slow_share = 0.35
    broad_share = 0.35
    slow = jnp.exp(jax.random.uniform(slow_key, (WIDTH, MODES), jnp.float32, math.log(0.25), math.log(2.0))) / LENGTH
    fast = jnp.exp(jax.random.uniform(fast_key, (WIDTH, MODES), jnp.float32, math.log(1.0 / 60.0), math.log(1.0 / 25.0)))
    broad_rate = jnp.exp(jax.random.uniform(broad_key, (WIDTH, MODES), jnp.float32, math.log(0.25 / LENGTH), math.log(0.04)))
    picked = jax.random.uniform(pick_key, (WIDTH, MODES), jnp.float32)
    return jnp.where(picked < slow_share, slow, jnp.where(picked < slow_share + broad_share, broad_rate, fast))


def draw_residue(key, part):
    key = jax.random.fold_in(key, 37)
    base_key, spread_key = jax.random.split(key, 2)
    column = jnp.arange(WIDTH, dtype=jnp.float32) / (WIDTH - 1)
    base = jnp.clip(jax.random.normal(base_key, (WIDTH, MODES), jnp.float32), -6.0, 6.0)
    rise = 1.0 + 2.0 * column
    spread = jnp.exp(jax.random.uniform(spread_key, (WIDTH,), jnp.float32, 0.0, math.log(10.0)))
    return base * (spread * jnp.sqrt(rise))[:, None] * MODES ** (-0.5)


def draw_gate_out(key, part):
    key = jax.random.fold_in(key, 53)
    base_key, spread_key = jax.random.split(key, 2)
    base = jnp.clip(jax.random.normal(base_key, (LENGTH, WIDTH), jnp.float32), -6.0, 6.0)
    spread = jnp.exp(jax.random.uniform(spread_key, (LENGTH,), jnp.float32, math.log(0.3), math.log(3.0)))
    return (base * spread[:, None]).astype(jnp.bfloat16)


def levels(rng, dims, shards, least, high):
    def one(position, parts):
        heights = jax.random.uniform(jax.random.fold_in(jax.random.fold_in(rng, 6), position), (parts,), jnp.float32, least / len(shards), high / len(shards))
        return jnp.repeat(jnp.exp(heights), dims[position] // parts).reshape((-1,) + (1,) * (len(dims) - position - 1))

    factor_of = one(*shards[0])
    for cut in shards[1:]:
        factor_of = factor_of * one(*cut)
    return factor_of


def bell_draw(own_key, dims, scale, limit, cuts=(), kind=jnp.bfloat16):
    gain = levels(own_key, dims, cuts, -0.22, 0.18) if cuts else 1.0
    values = jax.random.normal(own_key, dims, jnp.float32) * scale * gain
    return jnp.minimum(jnp.maximum(values, -limit), limit).astype(kind)


def setup_inputs(seed: int = 0) -> dict:
    keys = jax.random.split(jax.random.key(seed), 10)
    mixer_input = bell_draw(keys[0], (LENGTH, WIDTH), 1.0, 6.0, ((0, 32), (1, 4)))
    gate_in = bell_draw(keys[1], (LENGTH, WIDTH), 1.0, 6.0, ((0, 32), (1, 4)))
    gate_out = draw_gate_out(jax.random.fold_in(keys[9], 71), 0)
    residue = draw_residue(jax.random.fold_in(keys[9], 71), 0)
    decay_rate = draw_decay_rate(jax.random.fold_in(keys[9], 71), 0)
    norm_gain = jnp.clip(1.0 + 0.18 * jax.random.normal(keys[5], (WIDTH,), jnp.float32), 0.1, 1.9)
    queries = draw_queries(jax.random.fold_in(keys[9], 71), 0)
    key_vectors = draw_key_vectors(jax.random.fold_in(keys[9], 71), 0)
    grad_out = bell_draw(keys[8], (LENGTH, WIDTH), 1.0, 6.0, ((0, 32), (1, 4)))
    return dict(mixer_input=mixer_input, gate_in=gate_in, gate_out=gate_out, residue=residue, decay_rate=decay_rate, norm_gain=norm_gain, queries=queries, key_vectors=key_vectors, grad_out=grad_out)


EPS = 1e-06

def rounded(array):
    return lax.optimization_barrier(array.astype(jnp.bfloat16)).astype(jnp.float32)

def modal_filter(drive, decay, residue):

    def advance(state, row):
        state = decay * state + row[:, None]
        return (state, lax.optimization_barrier(jnp.sum(residue * state, axis=1)))
    start = jnp.zeros(decay.shape, jnp.float32)
    _, filtered = lax.scan(advance, start, drive)
    return filtered

def split_heads(rows):
    return rows.reshape(rows.shape[0], HEADS, HEAD_DIM).astype(jnp.float32)

def pair_scores(query_rows, key_rows, query_start, key_start):
    scale = 1.0 / math.sqrt(HEAD_DIM)
    scores = jnp.einsum('thd,shd->hts', split_heads(query_rows), split_heads(key_rows)) * scale
    query_place = query_start + jnp.arange(query_rows.shape[0], dtype=jnp.int32)
    key_place = key_start + jnp.arange(key_rows.shape[0], dtype=jnp.int32)
    allowed = (key_place[None, :] <= query_place[:, None]) & (key_place[None, :] >= 0)
    allowed = allowed & (query_place[:, None] < LENGTH)
    allowed = allowed & (query_place[:, None] // TOK_DEV - key_place[None, :] // TOK_DEV <= SPAN)
    return (scores, allowed)

def reference(mixer_input, gate_in, gate_out, residue, decay_rate, norm_gain, queries, key_vectors, grad_out):
    scale = 1.0 / math.sqrt(HEAD_DIM)
    decay = jnp.exp(-decay_rate)
    drive = gate_in.astype(jnp.float32) * mixer_input.astype(jnp.float32)
    gate = gate_out.astype(jnp.float32)
    mixed = gate * modal_filter(drive, decay, residue)
    inverse = lax.rsqrt(lax.optimization_barrier(jnp.mean(mixed * mixed, axis=1)) + EPS)
    values = (mixed * inverse[:, None] * norm_gain[None, :]).astype(jnp.bfloat16)
    margin = SPAN * TOK_DEV
    window = margin + TOK_DEV
    block_ids = jnp.arange(N_CTX, dtype=jnp.int32)
    keys_front = jnp.pad(key_vectors, ((margin, 0), (0, 0)))
    values_front = jnp.pad(values, ((margin, 0), (0, 0)))

    def forward_block(index):
        start = index * TOK_DEV
        query_rows = lax.dynamic_slice_in_dim(queries, start, TOK_DEV)
        key_rows = lax.dynamic_slice_in_dim(keys_front, start, window)
        value_rows = lax.dynamic_slice_in_dim(values_front, start, window)
        scores, allowed = pair_scores(query_rows, key_rows, start, start - margin)
        highest = lax.optimization_barrier(jnp.max(jnp.where(allowed[None], scores, -jnp.inf), axis=2))
        expo = jnp.where(allowed[None], jnp.exp(scores - highest[:, :, None]), 0.0)
        total = lax.optimization_barrier(jnp.sum(expo, axis=2))
        weights = rounded(expo / total[:, :, None])
        output = jnp.einsum('hts,shd->thd', weights, split_heads(value_rows))
        return (output.reshape(TOK_DEV, WIDTH).astype(jnp.bfloat16), highest + jnp.log(total))
    attended, log_total = lax.map(forward_block, block_ids)
    attended = attended.reshape(LENGTH, WIDTH)
    log_total = jnp.transpose(log_total, (0, 2, 1)).reshape(LENGTH, HEADS)
    delta = lax.optimization_barrier(jnp.sum(split_heads(grad_out) * split_heads(attended), axis=2))

    def query_block(index):
        start = index * TOK_DEV
        query_rows = lax.dynamic_slice_in_dim(queries, start, TOK_DEV)
        cotangent_rows = lax.dynamic_slice_in_dim(grad_out, start, TOK_DEV)
        key_rows = lax.dynamic_slice_in_dim(keys_front, start, window)
        value_rows = lax.dynamic_slice_in_dim(values_front, start, window)
        log_rows = jnp.transpose(lax.dynamic_slice_in_dim(log_total, start, TOK_DEV))
        delta_rows = jnp.transpose(lax.dynamic_slice_in_dim(delta, start, TOK_DEV))
        scores, allowed = pair_scores(query_rows, key_rows, start, start - margin)
        probs = jnp.where(allowed[None], jnp.exp(scores - log_rows[:, :, None]), 0.0)
        dprob = jnp.einsum('thd,shd->hts', split_heads(cotangent_rows), split_heads(value_rows))
        dscore = rounded(probs * (dprob - delta_rows[:, :, None]))
        grad_rows = jnp.einsum('hts,shd->thd', dscore, split_heads(key_rows)) * scale
        return grad_rows.reshape(TOK_DEV, WIDTH).astype(jnp.bfloat16)
    grad_queries = lax.map(query_block, block_ids).reshape(LENGTH, WIDTH)
    queries_back = jnp.pad(queries, ((0, margin), (0, 0)))
    cotangent_back = jnp.pad(grad_out, ((0, margin), (0, 0)))
    log_back = jnp.pad(log_total, ((0, margin), (0, 0)))
    delta_back = jnp.pad(delta, ((0, margin), (0, 0)))

    def key_block(index):
        start = index * TOK_DEV
        query_rows = lax.dynamic_slice_in_dim(queries_back, start, window)
        cotangent_rows = lax.dynamic_slice_in_dim(cotangent_back, start, window)
        key_rows = lax.dynamic_slice_in_dim(key_vectors, start, TOK_DEV)
        value_rows = lax.dynamic_slice_in_dim(values, start, TOK_DEV)
        log_rows = jnp.transpose(lax.dynamic_slice_in_dim(log_back, start, window))
        delta_rows = jnp.transpose(lax.dynamic_slice_in_dim(delta_back, start, window))
        scores, allowed = pair_scores(query_rows, key_rows, start, start)
        probs = jnp.where(allowed[None], jnp.exp(scores - log_rows[:, :, None]), 0.0)
        grad_value_rows = jnp.einsum('hts,thd->shd', rounded(probs), split_heads(cotangent_rows))
        dprob = jnp.einsum('thd,shd->hts', split_heads(cotangent_rows), split_heads(value_rows))
        dscore = rounded(probs * (dprob - delta_rows[:, :, None]))
        grad_key_rows = jnp.einsum('hts,thd->shd', dscore, split_heads(query_rows)) * scale
        return (grad_key_rows.reshape(TOK_DEV, WIDTH).astype(jnp.bfloat16), grad_value_rows.reshape(TOK_DEV, WIDTH))
    grad_keys, grad_values = lax.map(key_block, block_ids)
    grad_keys = grad_keys.reshape(LENGTH, WIDTH)
    grad_values = grad_values.reshape(LENGTH, WIDTH)
    scaled = norm_gain[None, :] * grad_values
    inner_dot = lax.optimization_barrier(jnp.sum(scaled * mixed, axis=1))
    grad_mixed = inverse[:, None] * scaled - mixed * (inverse ** 3 * inner_dot / WIDTH)[:, None]
    grad_drive = modal_filter((gate * grad_mixed)[::-1], decay, residue)[::-1]
    grad_input = (gate_in.astype(jnp.float32) * grad_drive).astype(jnp.bfloat16)
    return (attended, grad_queries, grad_keys, grad_input)
```

```python
import functools
import math

import jax
import jax.numpy as jnp
from jax import lax
from jax.experimental import pallas as pl
from jax.experimental.pallas import tpu as pltpu
from jax.sharding import PartitionSpec as P

HEAD_DIM = 128
SPAN = 2
EPS = 1e-06
LOG2E = 1.4426950408889634
MASKED = -1e30
LANES = 128
SUBLANES = 8
ROWS_PER_STEP = 8
f32 = jnp.float32
bf16 = jnp.bfloat16


def params(*semantics):
    return pltpu.CompilerParams(dimension_semantics=semantics or None, vmem_limit_bytes=48 << 20)


def shifted(value, by):
    devices = lax.axis_size("ctx")
    return lax.ppermute(value, "ctx", [(i, (i + by) % devices) for i in range(devices)])


def along(value, axis, by):
    def target(i):
        place = [i // 8, (i // 4) % 2, i % 4]
        size = (4, 2, 4)
        place[axis] = (place[axis] + by) % size[axis]
        return (place[0] * 2 + place[1]) * 4 + place[2]

    return lax.ppermute(value, "ctx", [(i, target(i)) for i in range(32)])


def carry_in(final, rate, length, reverse):
    position = lax.axis_index("ctx")
    position = (31 - position) if reverse else position
    sign = -1 if reverse else 1
    x, y, z = position // 8, (position // 4) % 2, position % 4

    def decayed(blocks, keep=True):
        blocks = jnp.asarray(blocks, f32)
        return jnp.where(keep, jnp.exp(-rate * (length * jnp.maximum(blocks, 0.0))), 0.0)

    others = [along(final, 2, sign * d) for d in (1, 2, 3)]
    state = sum(decayed(d - 1, d <= z) * other for d, other in zip((1, 2, 3), others))
    group = decayed(3 - z) * final
    for d, other in zip((1, 2, 3), others):
        group = group + decayed(3 - (z - d) % 4) * other
    partner = along(group, 1, 1)
    state = state + decayed(z, y == 1) * partner
    pair = jnp.where(y == 1, group + decayed(4) * partner, partner + decayed(4) * group)
    planes = [along(pair, 0, sign * d) for d in (1, 2, 3)]
    for d, other in zip((1, 2, 3), planes):
        state = state + decayed(position % 8 + 8 * (d - 1), d <= x) * other
    return state


def to_tokens(scratch, head, rows, block):
    scratch[pl.ds(head, rows, SUBLANES), :] = block


def from_tokens(scratch, head, rows):
    return scratch[pl.ds(head, rows, SUBLANES), :]


def head_slice(head):
    return slice(head * LANES, (head + 1) * LANES)


def tile(ref, m):
    return ref[m * SUBLANES : (m + 1) * SUBLANES, :]


def scan(drive, decay, residue, state, rows, out, reverse):
    modes = len(decay)

    def step(i, state):
        state = list(state)
        for j in range(ROWS_PER_STEP):
            t = i * ROWS_PER_STEP + j
            t = (rows - 1 - t) if reverse else t
            place = pl.ds(pl.multiple_of(t * SUBLANES, SUBLANES), SUBLANES)
            row = drive[place, :]
            state = [decay[m] * state[m] + row for m in range(modes)]
            if out is not None:
                terms = [residue[m] * state[m] for m in range(modes)]
                while len(terms) > 1:
                    terms = [a + b for a, b in zip(terms[::2], terms[1::2])]
                out[place, :] = terms[0]
        return tuple(state)

    return lax.fori_loop(0, rows // ROWS_PER_STEP, step, tuple(state))


def spread(source, target):
    modes, width = source.shape
    for head in range(width // LANES):
        to_tokens(target, head, modes, source[:, head_slice(head)])


def decays(rates, modes):
    return [jnp.exp(-tile(rates, m)) for m in range(modes)]


def forward_state_kernel(mixer, gate_in, rate, final, rates, drive):
    rows, width = mixer.shape
    modes = rate.shape[0]
    spread(rate, rates)
    for head in range(width // LANES):
        cut = head_slice(head)
        to_tokens(drive, head, rows, mixer[:, cut].astype(f32) * gate_in[:, cut].astype(f32))
    zero = jnp.zeros((SUBLANES, LANES), f32)
    state = scan(drive, decays(rates, modes), None, [zero] * modes, rows, None, False)
    for m in range(modes):
        final[m * SUBLANES : (m + 1) * SUBLANES, :] = state[m]


def forward_state(mixer, gate_in, rate):
    rows, width = mixer.shape
    modes = rate.shape[0]
    small = jax.ShapeDtypeStruct((modes * SUBLANES, LANES), f32)
    big = jax.ShapeDtypeStruct((rows * SUBLANES, LANES), f32)
    return pl.pallas_call(
        forward_state_kernel,
        out_shape=(small, small, big),
        compiler_params=params(),
        name="forward_state",
    )(mixer, gate_in, rate)


def row_total(block):
    ones = jnp.ones((SUBLANES, LANES), f32)
    return lax.dot_general(
        ones, block, (((1,), (1,)), ((), ())), precision=lax.Precision.HIGHEST, preferred_element_type=f32
    )


def forward_mix_kernel(drive, rates, residue, start, gate_out, gain, mixed, scaled, squares, residues, out):
    rows, width = mixed.shape
    modes = residue.shape[0]
    spread(residue, residues)
    decay = decays(rates, modes)
    res = [tile(residues, m) for m in range(modes)]
    scan(drive, decay, res, [tile(start, m) for m in range(modes)], rows, out, False)
    total = jnp.zeros((rows, LANES), f32)
    for head in range(width // LANES):
        cut = head_slice(head)
        value = gate_out[:, cut].astype(f32) * from_tokens(out, head, rows)
        mixed[:, cut] = value
        scaled[:, cut] = (value * gain[:, cut]).astype(bf16)
        total = total + value * value
    squares[...] = row_total(total)


def forward_mix(drive, rates, residue, start, gate_out, gain):
    rows, width = gate_out.shape
    modes = residue.shape[0]
    return pl.pallas_call(
        forward_mix_kernel,
        out_shape=(
            jax.ShapeDtypeStruct((rows, width), f32),
            jax.ShapeDtypeStruct((rows, width), bf16),
            jax.ShapeDtypeStruct((SUBLANES, rows), f32),
        ),
        scratch_shapes=[
            pltpu.VMEM((modes * SUBLANES, LANES), f32),
            pltpu.VMEM((rows * SUBLANES, LANES), f32),
        ],
        compiler_params=params(),
        name="forward_mix",
    )(drive, rates, residue, start, gate_out, gain)


def column(rows_ref):
    return jnp.transpose(rows_ref[...])[:, 0:1]


def inverse_of(squares, full_width):
    return lax.rsqrt(squares * (1.0 / full_width) + EPS)


def backward_state_kernel(full_width, scaled, mixed, gate_out, squares, inner, rates, final, drive):
    rows, width = mixed.shape
    modes = rates.shape[0] // SUBLANES
    inverse = inverse_of(column(squares), full_width)
    pull = inverse * inverse * inverse * column(inner) * (1.0 / full_width)
    for head in range(width // LANES):
        cut = head_slice(head)
        grad = inverse * scaled[:, cut] - mixed[:, cut] * pull
        to_tokens(drive, head, rows, gate_out[:, cut].astype(f32) * grad)
    zero = jnp.zeros((SUBLANES, LANES), f32)
    state = scan(drive, decays(rates, modes), None, [zero] * modes, rows, None, True)
    for m in range(modes):
        final[m * SUBLANES : (m + 1) * SUBLANES, :] = state[m]


def backward_state(full_width, scaled, mixed, gate_out, squares, inner, rates):
    rows, width = mixed.shape
    return pl.pallas_call(
        functools.partial(backward_state_kernel, full_width),
        out_shape=(
            jax.ShapeDtypeStruct(rates.shape, f32),
            jax.ShapeDtypeStruct((rows * SUBLANES, LANES), f32),
        ),
        compiler_params=params(),
        name="backward_state",
    )(scaled, mixed, gate_out, squares, inner, rates)


def backward_mix_kernel(drive, rates, residue, start, gate_in, grad, residues, out):
    rows, width = gate_in.shape
    modes = residue.shape[0]
    spread(residue, residues)
    decay = decays(rates, modes)
    res = [tile(residues, m) for m in range(modes)]
    scan(drive, decay, res, [tile(start, m) for m in range(modes)], rows, out, True)
    for head in range(width // LANES):
        cut = head_slice(head)
        grad[:, cut] = (gate_in[:, cut].astype(f32) * from_tokens(out, head, rows)).astype(bf16)


def backward_mix(drive, rates, residue, start, gate_in):
    rows, width = gate_in.shape
    modes = residue.shape[0]
    return pl.pallas_call(
        backward_mix_kernel,
        out_shape=jax.ShapeDtypeStruct((rows, width), bf16),
        scratch_shapes=[
            pltpu.VMEM((modes * SUBLANES, LANES), f32),
            pltpu.VMEM((rows * SUBLANES, LANES), f32),
        ],
        compiler_params=params(),
        name="backward_mix",
    )(drive, rates, residue, start, gate_in)


def rows_by_rows(a, b):
    return lax.dot_general(a, b, (((1,), (1,)), ((), ())), preferred_element_type=f32)


def product(a, b):
    return jnp.dot(a, b, preferred_element_type=f32)


def masked(scores, offset, near, transposed):
    if offset == 0:
        rows = lax.broadcasted_iota(jnp.int32, scores.shape, 0)
        columns = lax.broadcasted_iota(jnp.int32, scores.shape, 1)
        allowed = (rows <= columns) if transposed else (columns <= rows)
        return jnp.where(allowed, scores, MASKED)
    return scores + jnp.where(near, 0.0, MASKED)


SCALE = 1.0 / math.sqrt(HEAD_DIM)


def totals_kernel(place, queries, keys, keys_1, keys_2, totals):
    head = pl.program_id(0)
    position = place[0]
    scores = [
        masked(rows_by_rows(block[...], queries[...]) * (SCALE * LOG2E), offset, position >= offset, True)
        for offset, block in enumerate((keys, keys_1, keys_2))
    ]
    top = functools.reduce(jnp.maximum, [jnp.max(s, axis=0, keepdims=True) for s in scores])
    total = sum(jnp.sum(jnp.exp2(s - top), axis=0, keepdims=True) for s in scores)
    totals[pl.ds(head, 1), :] = top + jnp.log(total) * LOG2E


def head_block(rows, part=0):
    return pl.BlockSpec((rows, HEAD_DIM), lambda head, *_: (part, head))


def whole(shape):
    return pl.BlockSpec(shape, lambda head, *_: (0,) * len(shape))


def per_head(kernel, place, operands, specs, out_shape, out_specs, scratch=(), name=None):
    heads = operands[0].shape[1] // HEAD_DIM
    return pl.pallas_call(
        kernel,
        out_shape=out_shape,
        grid_spec=pltpu.PrefetchScalarGridSpec(
            num_scalar_prefetch=1,
            grid=(heads,),
            in_specs=specs,
            out_specs=out_specs,
            scratch_shapes=scratch,
        ),
        compiler_params=params("arbitrary"),
        name=name,
    )(place, *operands)


def row_totals(place, queries, keys, keys_1, keys_2):
    rows, width = queries.shape
    shape = (width // HEAD_DIM, rows)
    block = head_block(rows)
    return per_head(
        totals_kernel,
        place,
        (queries, keys, keys_1, keys_2),
        [block] * 4,
        jax.ShapeDtypeStruct(shape, f32),
        whole(shape),
        name="row_totals",
    )


def value_grads_kernel(
    blocks, place, keys, q0, q1, q2, d0, d1, d2, t0, t1, t2, gain, mixed, scaled, inner, acc
):
    head = pl.program_id(0)
    position = place[0]
    grad = None
    for offset, (query, cotangent, total) in enumerate(((q0, d0, t0), (q1, d1, t1), (q2, d2, t2))):
        scores = rows_by_rows(keys[...], query[...]) * (SCALE * LOG2E)
        scores = masked(scores, offset, position + offset < blocks, True)
        probs = jnp.exp2(scores - total[pl.ds(head, 1), :])
        part = product(probs.astype(bf16), cotangent[...])
        grad = part if grad is None else grad + part
    value = grad * gain[...]
    scaled[...] = value

    @pl.when(head == 0)
    def _():
        acc[...] = jnp.zeros_like(acc)

    acc[...] += value * mixed[...]

    @pl.when(head == pl.num_programs(0) - 1)
    def _():
        inner[...] = row_total(acc[...])


def value_grads(blocks, place, keys, queries, cotangents, totals, gain, mixed):
    rows, width = keys.shape
    heads = width // HEAD_DIM
    block = head_block(rows)
    stat = whole((heads, rows))
    return per_head(
        functools.partial(value_grads_kernel, blocks),
        place,
        (keys, *queries, *cotangents, *totals, gain, mixed),
        [block] * 7 + [stat] * 3 + [head_block(1), block],
        (jax.ShapeDtypeStruct((rows, width), f32), jax.ShapeDtypeStruct((SUBLANES, rows), f32)),
        (block, whole((SUBLANES, rows))),
        scratch=[pltpu.VMEM((rows, LANES), f32)],
        name="value_grads",
    )


def attend_kernel(
    full_width, place, queries, cotangent, k0, k1, k2, v0, v1, v2, s0, s1, s2, totals, attended, grad, delta, columns
):
    head = pl.program_id(0)
    position = place[0]

    @pl.when(head == 0)
    def _():
        columns[...] = jnp.transpose(totals[...])

    lane = lax.broadcasted_iota(jnp.int32, columns.shape, 1)
    log_total = jnp.sum(jnp.where(lane == head, columns[...], 0.0), axis=1, keepdims=True)
    probs, inverses = [], []
    output = None
    for offset, (key, value, squares) in enumerate(((k0, v0, s0), (k1, v1, s1), (k2, v2, s2))):
        scores = rows_by_rows(queries[...], key[...]) * (SCALE * LOG2E)
        scores = masked(scores, offset, position >= offset, False)
        prob = jnp.exp2(scores - log_total)
        inverse = inverse_of(squares[0:1, :], full_width)
        probs.append(prob)
        inverses.append(inverse)
        part = product((prob * inverse).astype(bf16), value[...])
        output = part if output is None else output + part
    result = output.astype(bf16)
    attended[...] = result
    weighed = cotangent[...].astype(f32) * result.astype(f32)
    delta[pl.ds(head, 1), :] = row_total(weighed)[0:1, :]
    delta_column = jnp.sum(weighed, axis=1, keepdims=True)
    total = None
    for prob, inverse, key, value in zip(probs, inverses, (k0, k1, k2), (v0, v1, v2)):
        dprob = rows_by_rows(cotangent[...], value[...]) * inverse
        dscore = (prob * (dprob - delta_column)).astype(bf16)
        part = product(dscore, key[...])
        total = part if total is None else total + part
    grad[...] = (total * SCALE).astype(bf16)


def attend(full_width, place, queries, cotangent, keys, values, squares, totals):
    rows, width = queries.shape
    heads = width // HEAD_DIM
    block = head_block(rows)
    stat = whole((heads, rows))
    out = jax.ShapeDtypeStruct((rows, width), bf16)
    return per_head(
        functools.partial(attend_kernel, full_width),
        place,
        (queries, cotangent, *keys, *values, *squares, totals),
        [block] * 8 + [whole((SUBLANES, rows))] * 3 + [stat],
        (out, out, jax.ShapeDtypeStruct((heads, rows), f32)),
        (block, block, stat),
        scratch=[pltpu.VMEM((rows, heads), f32)],
        name="attend",
    )


def key_grads_kernel(
    full_width, blocks, place, keys, values, q0, q1, q2, d0, d1, d2, t0, t1, t2, e0, e1, e2, squares, grad
):
    head = pl.program_id(0)
    position = place[0]
    inverse = inverse_of(column(squares), full_width)
    total = None
    groups = ((q0, d0, t0, e0), (q1, d1, t1, e1), (q2, d2, t2, e2))
    for offset, (query, cotangent, log_total, delta) in enumerate(groups):
        scores = rows_by_rows(keys[...], query[...]) * (SCALE * LOG2E)
        scores = masked(scores, offset, position + offset < blocks, True)
        probs = jnp.exp2(scores - log_total[pl.ds(head, 1), :])
        dprob = rows_by_rows(values[...], cotangent[...]) * inverse
        dscore = (probs * (dprob - delta[pl.ds(head, 1), :])).astype(bf16)
        part = product(dscore, query[...])
        total = part if total is None else total + part
    grad[...] = (total * SCALE).astype(bf16)


def key_grads(full_width, blocks, place, keys, values, queries, cotangents, totals, deltas, squares):
    rows, width = keys.shape
    heads = width // HEAD_DIM
    block = head_block(rows)
    stat = whole((heads, rows))
    return per_head(
        functools.partial(key_grads_kernel, full_width, blocks),
        place,
        (keys, values, *queries, *cotangents, *totals, *deltas, squares),
        [block] * 8 + [stat] * 6 + [whole((SUBLANES, rows))],
        jax.ShapeDtypeStruct((rows, width), bf16),
        block,
        name="key_grads",
    )


def shards(
    mixer_input, gate_in, gate_out, residue, decay_rate, norm_gain, queries, key_vectors, grad_out
):
    length, width = queries.shape
    full_width = width * lax.axis_size("tp")
    blocks = lax.axis_size("ctx")
    place = lax.axis_index("ctx").reshape(1).astype(jnp.int32)
    gain = norm_gain[None, :]
    residue = jnp.transpose(residue)

    keys_1 = shifted(key_vectors, 1)
    keys_2 = shifted(keys_1, 1)
    queries_1 = shifted(queries, -1)
    cotangent_1 = shifted(grad_out, -1)
    queries_2 = shifted(queries_1, -1)
    cotangent_2 = shifted(cotangent_1, -1)

    final, rates, drive = forward_state(mixer_input, gate_in, jnp.transpose(decay_rate))
    start = carry_in(final, rates, length, False)
    mixed, scaled_mix, squares = forward_mix(drive, rates, residue, start, gate_out, gain)
    mix_1 = shifted(scaled_mix, 1)
    mix_2 = shifted(mix_1, 1)
    squares = lax.psum(squares, "tp")
    squares_1 = shifted(squares, 1)
    squares_2 = shifted(squares, 2)

    totals = row_totals(place, queries, key_vectors, keys_1, keys_2)
    totals_1 = shifted(totals, -1)
    totals_2 = shifted(totals, -2)
    all_queries = (queries, queries_1, queries_2)
    all_cotangents = (grad_out, cotangent_1, cotangent_2)
    all_totals = (totals, totals_1, totals_2)
    scaled, inner = value_grads(
        blocks, place, key_vectors, all_queries, all_cotangents, all_totals, gain, mixed
    )
    inner = lax.psum(inner, "tp")
    final, drive = backward_state(full_width, scaled, mixed, gate_out, squares, inner, rates)
    start = carry_in(final, rates, length, True)
    grad_input = backward_mix(drive, rates, residue, start, gate_in)

    attended, grad_queries, delta = attend(
        full_width,
        place,
        queries,
        grad_out,
        (key_vectors, keys_1, keys_2),
        (scaled_mix, mix_1, mix_2),
        (squares, squares_1, squares_2),
        totals,
    )
    all_deltas = (delta, shifted(delta, -1), shifted(delta, -2))
    grad_keys = key_grads(
        full_width,
        blocks,
        place,
        key_vectors,
        scaled_mix,
        all_queries,
        all_cotangents,
        all_totals,
        all_deltas,
        squares,
    )
    return (attended, grad_queries, grad_keys, grad_input)


def solution(mesh):
    in_specs = (
        P("ctx", "tp"),
        P("ctx", "tp"),
        P("ctx", "tp"),
        P("tp", None),
        P("tp", None),
        P("tp"),
        P("ctx", "tp"),
        P("ctx", "tp"),
        P("ctx", "tp"),
    )
    out_specs = (P("ctx", "tp"), P("ctx", "tp"), P("ctx", "tp"), P("ctx", "tp"))
    return jax.shard_map(shards, mesh=mesh, in_specs=in_specs, out_specs=out_specs, check_vma=False)
```

```python
import functools
import math

import jax
import jax.numpy as jnp
from jax import lax
from jax.experimental import pallas as pl
from jax.experimental.pallas import tpu as pltpu
from jax.sharding import PartitionSpec as P

HEAD_DIM = 128
SPAN = 2
EPS = 1e-06
LOG2E = 1.4426950408889634
MASKED = -1e30
LANES = 128
SUBLANES = 8
ROWS_PER_STEP = 8
HEADS_PER_STEP = 4
GROUP = HEADS_PER_STEP * HEAD_DIM
f32 = jnp.float32
bf16 = jnp.bfloat16


COST = 0.3


def cost(microseconds):
    microseconds = microseconds * COST
    return pl.CostEstimate(
        flops=int(microseconds * 1.0e9), bytes_accessed=int(microseconds * 2.0e6), transcendentals=0
    )


def params(*semantics):
    return pltpu.CompilerParams(dimension_semantics=semantics or None, vmem_limit_bytes=48 << 20)


def shifted(value, by):
    devices = lax.axis_size("ctx")
    return lax.ppermute(value, "ctx", [(i, (i + by) % devices) for i in range(devices)])


def along(value, axis, by):
    def target(i):
        place = [i // 8, (i // 4) % 2, i % 4]
        size = (4, 2, 4)
        place[axis] = (place[axis] + by) % size[axis]
        return (place[0] * 2 + place[1]) * 4 + place[2]

    return lax.ppermute(value, "ctx", [(i, target(i)) for i in range(32)])


def carry_in(final, rate, length, reverse):
    position = lax.axis_index("ctx")
    position = (31 - position) if reverse else position
    sign = -1 if reverse else 1
    x, y, z = position // 8, (position // 4) % 2, position % 4

    def decayed(blocks, keep=True):
        blocks = jnp.asarray(blocks, f32)
        return jnp.where(keep, jnp.exp(-rate * (length * jnp.maximum(blocks, 0.0))), 0.0)

    others = [along(final, 2, sign * d) for d in (1, 2, 3)]
    state = sum(decayed(d - 1, d <= z) * other for d, other in zip((1, 2, 3), others))
    group = decayed(3 - z) * final
    for d, other in zip((1, 2, 3), others):
        group = group + decayed(3 - (z - d) % 4) * other
    partner = along(group, 1, 1)
    state = state + decayed(z, y == 1) * partner
    pair = jnp.where(y == 1, group + decayed(4) * partner, partner + decayed(4) * group)
    planes = [along(pair, 0, sign * d) for d in (1, 2, 3)]
    return (state, *planes)


def add_planes(place, reverse, length, rates, start, planes, target):
    position = (31 - place[0]) if reverse else place[0]
    state = start[...]
    for d, plane in zip((1, 2, 3), planes):
        blocks = (position % 8 + 8 * (d - 1)).astype(f32)
        factor = jnp.exp(-rates[...] * (blocks * length))
        state = state + plane[...] * jnp.where(position >= 8 * d, factor, 0.0)
    target[...] = state


def to_tokens(scratch, head, rows, block):
    scratch[pl.ds(head, rows, SUBLANES), :] = block


def from_tokens(scratch, head, rows):
    return scratch[pl.ds(head, rows, SUBLANES), :]


def head_slice(head):
    return slice(head * LANES, (head + 1) * LANES)


def tile(ref, m):
    return ref[m * SUBLANES : (m + 1) * SUBLANES, :]


def scan(drive, decay, residue, state, rows, out, reverse):
    modes = len(decay)

    def step(i, state):
        state = list(state)
        for j in range(ROWS_PER_STEP):
            t = i * ROWS_PER_STEP + j
            t = (rows - 1 - t) if reverse else t
            place = pl.ds(pl.multiple_of(t * SUBLANES, SUBLANES), SUBLANES)
            row = drive[place, :]
            state = [decay[m] * state[m] + row for m in range(modes)]
            if out is not None:
                terms = [residue[m] * state[m] for m in range(modes)]
                while len(terms) > 1:
                    terms = [a + b for a, b in zip(terms[::2], terms[1::2])]
                out[place, :] = terms[0]
        return tuple(state)

    return lax.fori_loop(0, rows // ROWS_PER_STEP, step, tuple(state))


def spread(source, target):
    modes, width = source.shape
    for head in range(width // LANES):
        to_tokens(target, head, modes, source[:, head_slice(head)])


def decays(rates, modes):
    return [jnp.exp(-tile(rates, m)) for m in range(modes)]


def forward_state_kernel(mixer, gate_in, rate, final, rates, drive):
    rows, width = mixer.shape
    modes = rate.shape[0]
    spread(rate, rates)
    for head in range(width // LANES):
        cut = head_slice(head)
        to_tokens(drive, head, rows, mixer[:, cut].astype(f32) * gate_in[:, cut].astype(f32))
    zero = jnp.zeros((SUBLANES, LANES), f32)
    state = scan(drive, decays(rates, modes), None, [zero] * modes, rows, None, False)
    for m in range(modes):
        final[m * SUBLANES : (m + 1) * SUBLANES, :] = state[m]


def forward_state(mixer, gate_in, rate):
    rows, width = mixer.shape
    modes = rate.shape[0]
    small = jax.ShapeDtypeStruct((modes * SUBLANES, LANES), f32)
    big = jax.ShapeDtypeStruct((rows * SUBLANES, LANES), f32)
    return pl.pallas_call(
        forward_state_kernel,
        out_shape=(small, small, big),
        compiler_params=params(),
        cost_estimate=cost(2),
        name="forward_state",
    )(mixer, gate_in, rate)


def row_total(block):
    ones = jnp.ones((SUBLANES, LANES), f32)
    totals = lax.dot_general(
        ones, block, (((1,), (1,)), ((), ())), precision=lax.Precision.HIGHEST, preferred_element_type=f32
    )
    return totals[0:1, :]


def forward_mix_kernel(
    place, drive, rates, residue, start, p1, p2, p3, gate_out, gain, mixed, scaled, squares, residues, out, carried
):
    rows, width = mixed.shape
    modes = residue.shape[0]
    spread(residue, residues)
    decay = decays(rates, modes)
    res = [tile(residues, m) for m in range(modes)]
    add_planes(place, False, rows, rates, start, (p1, p2, p3), carried)
    scan(drive, decay, res, [tile(carried, m) for m in range(modes)], rows, out, False)
    total = jnp.zeros((rows, LANES), f32)
    for head in range(width // LANES):
        cut = head_slice(head)
        value = gate_out[:, cut].astype(f32) * from_tokens(out, head, rows)
        mixed[:, cut] = value
        scaled[:, cut] = (value * gain[:, cut]).astype(bf16)
        total = total + value * value
    squares[...] = row_total(total)


def forward_mix(place, drive, rates, residue, carry, gate_out, gain):
    rows, width = gate_out.shape
    modes = residue.shape[0]
    return pl.pallas_call(
        forward_mix_kernel,
        out_shape=(
            jax.ShapeDtypeStruct((rows, width), f32),
            jax.ShapeDtypeStruct((rows, width), bf16),
            jax.ShapeDtypeStruct((1, rows), f32),
        ),
        scratch_shapes=[
            pltpu.VMEM((modes * SUBLANES, LANES), f32),
            pltpu.VMEM((rows * SUBLANES, LANES), f32),
            pltpu.VMEM((modes * SUBLANES, LANES), f32),
        ],
        in_specs=[pl.BlockSpec(memory_space=pltpu.SMEM)] + [pl.BlockSpec(memory_space=pltpu.VMEM)] * 9,
        compiler_params=params(),
        cost_estimate=cost(4),
        name="forward_mix",
    )(place, drive, rates, residue, *carry, gate_out, gain)


def column(row):
    return jnp.transpose(jnp.broadcast_to(row, (SUBLANES, row.shape[1])))[:, 0:1]


def inverse_of(squares, full_width):
    return lax.rsqrt(squares * (1.0 / full_width) + EPS)


def backward_state_kernel(full_width, scaled, mixed, gate_out, stats, rates, final, drive):
    rows, width = mixed.shape
    modes = rates.shape[0] // SUBLANES
    inverse = inverse_of(column(stats[0:1, :]), full_width)
    pull = inverse * inverse * inverse * column(stats[1:2, :]) * (1.0 / full_width)
    for head in range(width // LANES):
        cut = head_slice(head)
        grad = inverse * scaled[:, cut] - mixed[:, cut] * pull
        to_tokens(drive, head, rows, gate_out[:, cut].astype(f32) * grad)
    zero = jnp.zeros((SUBLANES, LANES), f32)
    state = scan(drive, decays(rates, modes), None, [zero] * modes, rows, None, True)
    for m in range(modes):
        final[m * SUBLANES : (m + 1) * SUBLANES, :] = state[m]


def backward_state(full_width, scaled, mixed, gate_out, stats, rates):
    rows, width = mixed.shape
    return pl.pallas_call(
        functools.partial(backward_state_kernel, full_width),
        out_shape=(
            jax.ShapeDtypeStruct(rates.shape, f32),
            jax.ShapeDtypeStruct((rows * SUBLANES, LANES), f32),
        ),
        compiler_params=params(),
        cost_estimate=cost(2),
        name="backward_state",
    )(scaled, mixed, gate_out, stats, rates)


def backward_mix_kernel(place, drive, rates, residue, start, p1, p2, p3, gate_in, grad, residues, out, carried):
    rows, width = gate_in.shape
    modes = residue.shape[0]
    spread(residue, residues)
    decay = decays(rates, modes)
    res = [tile(residues, m) for m in range(modes)]
    add_planes(place, True, rows, rates, start, (p1, p2, p3), carried)
    scan(drive, decay, res, [tile(carried, m) for m in range(modes)], rows, out, True)
    for head in range(width // LANES):
        cut = head_slice(head)
        grad[:, cut] = (gate_in[:, cut].astype(f32) * from_tokens(out, head, rows)).astype(bf16)


def backward_mix(place, drive, rates, residue, carry, gate_in):
    rows, width = gate_in.shape
    modes = residue.shape[0]
    return pl.pallas_call(
        backward_mix_kernel,
        out_shape=jax.ShapeDtypeStruct((rows, width), bf16),
        scratch_shapes=[
            pltpu.VMEM((modes * SUBLANES, LANES), f32),
            pltpu.VMEM((rows * SUBLANES, LANES), f32),
            pltpu.VMEM((modes * SUBLANES, LANES), f32),
        ],
        in_specs=[pl.BlockSpec(memory_space=pltpu.SMEM)] + [pl.BlockSpec(memory_space=pltpu.VMEM)] * 8,
        compiler_params=params(),
        cost_estimate=cost(4),
        name="backward_mix",
    )(place, drive, rates, residue, *carry, gate_in)


def rows_by_rows(a, b):
    return lax.dot_general(a, b, (((1,), (1,)), ((), ())), preferred_element_type=f32)


def product(a, b):
    return jnp.dot(a, b, preferred_element_type=f32)


def masked(scores, offset, near, transposed):
    if offset == 0:
        rows = lax.broadcasted_iota(jnp.int32, scores.shape, 0)
        columns = lax.broadcasted_iota(jnp.int32, scores.shape, 1)
        allowed = (rows <= columns) if transposed else (columns <= rows)
        return jnp.where(allowed, scores, MASKED)
    return scores + jnp.where(near, 0.0, MASKED)


SCALE = 1.0 / math.sqrt(HEAD_DIM)


def step_heads():
    first = pl.program_id(0) * HEADS_PER_STEP
    return [(first + j, head_slice(j)) for j in range(HEADS_PER_STEP)]


def totals_kernel(place, queries, keys, keys_1, keys_2, totals):
    position = place[0]
    for head, cut in step_heads():
        scores = [
            masked(
                rows_by_rows(block[:, cut], queries[:, cut]) * (SCALE * LOG2E), offset, position >= offset, True
            )
            for offset, block in enumerate((keys, keys_1, keys_2))
        ]
        top = functools.reduce(jnp.maximum, [jnp.max(s, axis=0, keepdims=True) for s in scores])
        total = sum(jnp.sum(jnp.exp2(s - top), axis=0, keepdims=True) for s in scores)
        totals[pl.ds(head, 1), :] = top + jnp.log(total) * LOG2E


def head_block(rows):
    return pl.BlockSpec((rows, GROUP), lambda step, *_: (0, step))


def whole(shape):
    return pl.BlockSpec(shape, lambda head, *_: (0,) * len(shape))


def per_head(kernel, place, operands, specs, out_shape, out_specs, scratch=(), name=None, time=5):
    heads = operands[0].shape[1] // GROUP
    return pl.pallas_call(
        kernel,
        out_shape=out_shape,
        grid_spec=pltpu.PrefetchScalarGridSpec(
            num_scalar_prefetch=1,
            grid=(heads,),
            in_specs=specs,
            out_specs=out_specs,
            scratch_shapes=scratch,
        ),
        compiler_params=params("arbitrary"),
        cost_estimate=cost(time),
        name=name,
    )(place, *operands)


def row_totals(place, queries, keys, keys_1, keys_2):
    rows, width = queries.shape
    shape = (width // HEAD_DIM, rows)
    block = head_block(rows)
    return per_head(
        totals_kernel,
        place,
        (queries, keys, keys_1, keys_2),
        [block] * 4,
        jax.ShapeDtypeStruct(shape, f32),
        whole(shape),
        name="row_totals",
        time=4,
    )


def value_grads_kernel(
    blocks, place, keys, q0, q1, q2, d0, d1, d2, t0, t1, t2, gain, mixed, squares, scaled, stats, acc
):
    step = pl.program_id(0)
    position = place[0]

    @pl.when(step == 0)
    def _():
        acc[...] = jnp.zeros_like(acc)

    for head, cut in step_heads():
        grad = None
        for offset, (query, cotangent, total) in enumerate(((q0, d0, t0), (q1, d1, t1), (q2, d2, t2))):
            scores = rows_by_rows(keys[:, cut], query[:, cut]) * (SCALE * LOG2E)
            scores = masked(scores, offset, position + offset < blocks, True)
            probs = jnp.exp2(scores - total[pl.ds(head, 1), :])
            part = product(probs.astype(bf16), cotangent[:, cut])
            grad = part if grad is None else grad + part
        value = grad * gain[:, cut]
        scaled[:, cut] = value
        acc[...] += value * mixed[:, cut]

    @pl.when(step == pl.num_programs(0) - 1)
    def _():
        stats[0:1, :] = squares[...]
        stats[1:2, :] = row_total(acc[...])


def value_grads(blocks, place, keys, queries, cotangents, totals, gain, mixed, squares):
    rows, width = keys.shape
    heads = width // HEAD_DIM
    block = head_block(rows)
    stat = whole((heads, rows))
    return per_head(
        functools.partial(value_grads_kernel, blocks),
        place,
        (keys, *queries, *cotangents, *totals, gain, mixed, squares),
        [block] * 7 + [stat] * 3 + [head_block(1), block, whole((1, rows))],
        (jax.ShapeDtypeStruct((rows, width), f32), jax.ShapeDtypeStruct((2, rows), f32)),
        (block, whole((2, rows))),
        scratch=[pltpu.VMEM((rows, LANES), f32)],
        name="value_grads",
        time=7,
    )


def attend_kernel(
    full_width, place, queries, cotangent, k0, k1, k2, v0, v1, v2, s0, s1, s2, totals, attended, grad, delta, columns
):
    position = place[0]

    @pl.when(pl.program_id(0) == 0)
    def _():
        columns[...] = jnp.transpose(totals[...])

    lane = lax.broadcasted_iota(jnp.int32, columns.shape, 1)
    inverses = [inverse_of(squares[0:1, :], full_width) for squares in (s0, s1, s2)]
    for head, cut in step_heads():
        log_total = jnp.sum(jnp.where(lane == head, columns[...], 0.0), axis=1, keepdims=True)
        probs = []
        output = None
        for offset, (key, value) in enumerate(((k0, v0), (k1, v1), (k2, v2))):
            scores = rows_by_rows(queries[:, cut], key[:, cut]) * (SCALE * LOG2E)
            scores = masked(scores, offset, position >= offset, False)
            prob = jnp.exp2(scores - log_total)
            probs.append(prob)
            part = product((prob * inverses[offset]).astype(bf16), value[:, cut])
            output = part if output is None else output + part
        result = output.astype(bf16)
        attended[:, cut] = result
        weighed = cotangent[:, cut].astype(f32) * result.astype(f32)
        delta[pl.ds(head, 1), :] = row_total(weighed)
        delta_column = jnp.sum(weighed, axis=1, keepdims=True)
        total = None
        for prob, inverse, key, value in zip(probs, inverses, (k0, k1, k2), (v0, v1, v2)):
            dprob = rows_by_rows(cotangent[:, cut], value[:, cut]) * inverse
            dscore = (prob * (dprob - delta_column)).astype(bf16)
            part = product(dscore, key[:, cut])
            total = part if total is None else total + part
        grad[:, cut] = (total * SCALE).astype(bf16)


def attend(full_width, place, queries, cotangent, keys, values, squares, totals):
    rows, width = queries.shape
    heads = width // HEAD_DIM
    block = head_block(rows)
    stat = whole((heads, rows))
    out = jax.ShapeDtypeStruct((rows, width), bf16)
    return per_head(
        functools.partial(attend_kernel, full_width),
        place,
        (queries, cotangent, *keys, *values, *squares, totals),
        [block] * 8 + [whole((2, rows))] * 3 + [stat],
        (out, out, jax.ShapeDtypeStruct((heads, rows), f32)),
        (block, block, stat),
        scratch=[pltpu.VMEM((rows, heads), f32)],
        name="attend",
        time=10,
    )


def key_grads_kernel(
    full_width, blocks, place, keys, values, q0, q1, q2, d0, d1, d2, t0, t1, t2, e0, e1, e2, squares, grad
):
    position = place[0]
    inverse = inverse_of(column(squares[0:1, :]), full_width)
    groups = ((q0, d0, t0, e0), (q1, d1, t1, e1), (q2, d2, t2, e2))
    for head, cut in step_heads():
        total = None
        for offset, (query, cotangent, log_total, delta) in enumerate(groups):
            scores = rows_by_rows(keys[:, cut], query[:, cut]) * (SCALE * LOG2E)
            scores = masked(scores, offset, position + offset < blocks, True)
            probs = jnp.exp2(scores - log_total[pl.ds(head, 1), :])
            dprob = rows_by_rows(values[:, cut], cotangent[:, cut]) * inverse
            dscore = (probs * (dprob - delta[pl.ds(head, 1), :])).astype(bf16)
            part = product(dscore, query[:, cut])
            total = part if total is None else total + part
        grad[:, cut] = (total * SCALE).astype(bf16)


def key_grads(full_width, blocks, place, keys, values, queries, cotangents, totals, deltas, squares):
    rows, width = keys.shape
    heads = width // HEAD_DIM
    block = head_block(rows)
    stat = whole((heads, rows))
    return per_head(
        functools.partial(key_grads_kernel, full_width, blocks),
        place,
        (keys, values, *queries, *cotangents, *totals, *deltas, squares),
        [block] * 8 + [stat] * 6 + [whole((2, rows))],
        jax.ShapeDtypeStruct((rows, width), bf16),
        block,
        name="key_grads",
        time=8,
    )


def shards(
    mixer_input, gate_in, gate_out, residue, decay_rate, norm_gain, queries, key_vectors, grad_out
):
    length, width = queries.shape
    full_width = width * lax.axis_size("tp")
    blocks = lax.axis_size("ctx")
    place = lax.axis_index("ctx").reshape(1).astype(jnp.int32)
    gain = norm_gain[None, :]
    residue = jnp.transpose(residue)

    keys_1 = shifted(key_vectors, 1)
    keys_2 = shifted(keys_1, 1)
    queries_1 = shifted(queries, -1)
    cotangent_1 = shifted(grad_out, -1)
    queries_2 = shifted(queries_1, -1)
    cotangent_2 = shifted(cotangent_1, -1)

    final, rates, drive = forward_state(mixer_input, gate_in, jnp.transpose(decay_rate))
    carry = carry_in(final, rates, length, False)
    mixed, scaled_mix, squares = forward_mix(place, drive, rates, residue, carry, gate_out, gain)
    mix_1 = shifted(scaled_mix, 1)
    mix_2 = shifted(mix_1, 1)

    totals = row_totals(place, queries, key_vectors, keys_1, keys_2)
    totals_1 = shifted(totals, -1)
    totals_2 = shifted(totals, -2)
    all_queries = (queries, queries_1, queries_2)
    all_cotangents = (grad_out, cotangent_1, cotangent_2)
    all_totals = (totals, totals_1, totals_2)
    scaled, stats = value_grads(
        blocks, place, key_vectors, all_queries, all_cotangents, all_totals, gain, mixed, squares
    )
    stats = lax.psum(stats, "tp")
    stats_1 = shifted(stats, 1)
    stats_2 = shifted(stats, 2)
    final, drive = backward_state(full_width, scaled, mixed, gate_out, stats, rates)
    carry = carry_in(final, rates, length, True)
    grad_input = backward_mix(place, drive, rates, residue, carry, gate_in)

    attended, grad_queries, delta = attend(
        full_width,
        place,
        queries,
        grad_out,
        (key_vectors, keys_1, keys_2),
        (scaled_mix, mix_1, mix_2),
        (stats, stats_1, stats_2),
        totals,
    )
    all_deltas = (delta, shifted(delta, -1), shifted(delta, -2))
    grad_keys = key_grads(
        full_width,
        blocks,
        place,
        key_vectors,
        scaled_mix,
        all_queries,
        all_cotangents,
        all_totals,
        all_deltas,
        stats,
    )
    return (attended, grad_queries, grad_keys, grad_input)


def solution(mesh):
    in_specs = (
        P("ctx", "tp"),
        P("ctx", "tp"),
        P("ctx", "tp"),
        P("tp", None),
        P("tp", None),
        P("tp"),
        P("ctx", "tp"),
        P("ctx", "tp"),
        P("ctx", "tp"),
    )
    out_specs = (P("ctx", "tp"), P("ctx", "tp"), P("ctx", "tp"), P("ctx", "tp"))
    return jax.shard_map(shards, mesh=mesh, in_specs=in_specs, out_specs=out_specs, check_vma=False)
```

```python
import functools
import math

import jax
import jax.numpy as jnp
from jax import lax
from jax.experimental import pallas as pl
from jax.experimental.pallas import tpu as pltpu
from jax.sharding import PartitionSpec as P

HEAD_DIM = 128
SPAN = 2
EPS = 1e-06
LOG2E = 1.4426950408889634
MASKED = -1e30
LANES = 128
SUBLANES = 8
ROWS_PER_STEP = 8
HEADS_PER_STEP = 4
GROUP = HEADS_PER_STEP * HEAD_DIM
f32 = jnp.float32
bf16 = jnp.bfloat16


COST = 0.3


def cost(microseconds):
    microseconds = microseconds * COST
    return pl.CostEstimate(
        flops=int(microseconds * 1.0e9), bytes_accessed=int(microseconds * 2.0e6), transcendentals=0
    )


def params(*semantics, vmem=48):
    return pltpu.CompilerParams(dimension_semantics=semantics or None, vmem_limit_bytes=vmem << 20)


def shifted(value, by):
    devices = lax.axis_size("ctx")
    return lax.ppermute(value, "ctx", [(i, (i + by) % devices) for i in range(devices)])


def along(value, axis, by):
    def target(i):
        place = [i // 8, (i // 4) % 2, i % 4]
        size = (4, 2, 4)
        place[axis] = (place[axis] + by) % size[axis]
        return (place[0] * 2 + place[1]) * 4 + place[2]

    return lax.ppermute(value, "ctx", [(i, target(i)) for i in range(32)])


def carry_in(final, rate, length, reverse):
    position = lax.axis_index("ctx")
    position = (31 - position) if reverse else position
    sign = -1 if reverse else 1
    x, y, z = position // 8, (position // 4) % 2, position % 4

    def decayed(blocks, keep=True):
        blocks = jnp.asarray(blocks, f32)
        return jnp.where(keep, jnp.exp(-rate * (length * jnp.maximum(blocks, 0.0))), 0.0)

    others = [along(final, 2, sign * d) for d in (1, 2, 3)]
    state = sum(decayed(d - 1, d <= z) * other for d, other in zip((1, 2, 3), others))
    group = decayed(3 - z) * final
    for d, other in zip((1, 2, 3), others):
        group = group + decayed(3 - (z - d) % 4) * other
    partner = along(group, 1, 1)
    state = state + decayed(z, y == 1) * partner
    pair = jnp.where(y == 1, group + decayed(4) * partner, partner + decayed(4) * group)
    planes = [along(pair, 0, sign * d) for d in (1, 2, 3)]
    return (state, *planes)


def add_planes(place, reverse, length, rates, start, planes, target):
    position = (31 - place[0]) if reverse else place[0]
    state = start[...]
    for d, plane in zip((1, 2, 3), planes):
        blocks = (position % 8 + 8 * (d - 1)).astype(f32)
        factor = jnp.exp(-rates[...] * (blocks * length))
        state = state + plane[...] * jnp.where(position >= 8 * d, factor, 0.0)
    target[...] = state


def to_tokens(scratch, head, rows, block):
    scratch[pl.ds(head, rows, SUBLANES), :] = block


def from_tokens(scratch, head, rows):
    return scratch[pl.ds(head, rows, SUBLANES), :]


def head_slice(head):
    return slice(head * LANES, (head + 1) * LANES)


def tile(ref, m):
    return ref[m * SUBLANES : (m + 1) * SUBLANES, :]


def scan(drive, decay, residue, state, rows, out, reverse):
    modes = len(decay)

    def step(i, state):
        state = list(state)
        for j in range(ROWS_PER_STEP):
            t = i * ROWS_PER_STEP + j
            t = (rows - 1 - t) if reverse else t
            place = pl.ds(pl.multiple_of(t * SUBLANES, SUBLANES), SUBLANES)
            row = drive[place, :]
            state = [decay[m] * state[m] + row for m in range(modes)]
            if out is not None:
                terms = [residue[m] * state[m] for m in range(modes)]
                while len(terms) > 1:
                    terms = [a + b for a, b in zip(terms[::2], terms[1::2])]
                out[place, :] = terms[0]
        return tuple(state)

    return lax.fori_loop(0, rows // ROWS_PER_STEP, step, tuple(state))


def spread(source, target):
    modes, width = source.shape
    for head in range(width // LANES):
        to_tokens(target, head, modes, source[:, head_slice(head)])


def decays(rates, modes):
    return [jnp.exp(-tile(rates, m)) for m in range(modes)]


def form_drive(mixer, gate_in, drive):
    rows, width = mixer.shape
    for head in range(width // LANES):
        cut = head_slice(head)
        to_tokens(drive, head, rows, mixer[:, cut].astype(f32) * gate_in[:, cut].astype(f32))


def forward_state_kernel(mixer, gate_in, rate, final, rates, drive):
    rows, width = mixer.shape
    modes = rate.shape[0]
    spread(rate, rates)
    form_drive(mixer, gate_in, drive)
    zero = jnp.zeros((SUBLANES, LANES), f32)
    state = scan(drive, decays(rates, modes), None, [zero] * modes, rows, None, False)
    for m in range(modes):
        final[m * SUBLANES : (m + 1) * SUBLANES, :] = state[m]


def forward_state(mixer, gate_in, rate):
    rows, width = mixer.shape
    modes = rate.shape[0]
    small = jax.ShapeDtypeStruct((modes * SUBLANES, LANES), f32)
    return pl.pallas_call(
        forward_state_kernel,
        out_shape=(small, small),
        scratch_shapes=[pltpu.VMEM((rows * SUBLANES, LANES), f32)],
        compiler_params=params(),
        cost_estimate=cost(2),
        name="forward_state",
    )(mixer, gate_in, rate)


def row_total(block):
    ones = jnp.ones((SUBLANES, LANES), f32)
    totals = lax.dot_general(
        ones, block, (((1,), (1,)), ((), ())), precision=lax.Precision.HIGHEST, preferred_element_type=f32
    )
    return totals[0:1, :]


def forward_mix_kernel(
    place,
    mixer,
    gate_in,
    rates,
    residue,
    start,
    p1,
    p2,
    p3,
    gate_out,
    gain,
    mixed,
    scaled,
    squares,
    residues,
    out,
    carried,
    drive,
):
    rows, width = mixed.shape
    modes = residue.shape[0]
    spread(residue, residues)
    decay = decays(rates, modes)
    res = [tile(residues, m) for m in range(modes)]
    form_drive(mixer, gate_in, drive)
    add_planes(place, False, rows, rates, start, (p1, p2, p3), carried)
    scan(drive, decay, res, [tile(carried, m) for m in range(modes)], rows, out, False)
    total = jnp.zeros((rows, LANES), f32)
    for head in range(width // LANES):
        cut = head_slice(head)
        value = gate_out[:, cut].astype(f32) * from_tokens(out, head, rows)
        mixed[:, cut] = value
        scaled[:, cut] = (value * gain[:, cut]).astype(bf16)
        total = total + value * value
    squares[...] = row_total(total)


def forward_mix(place, mixer, gate_in, rates, residue, carry, gate_out, gain):
    rows, width = gate_out.shape
    modes = residue.shape[0]
    return pl.pallas_call(
        forward_mix_kernel,
        out_shape=(
            jax.ShapeDtypeStruct((rows, width), f32),
            jax.ShapeDtypeStruct((rows, width), bf16),
            jax.ShapeDtypeStruct((1, rows), f32),
        ),
        scratch_shapes=[
            pltpu.VMEM((modes * SUBLANES, LANES), f32),
            pltpu.VMEM((rows * SUBLANES, LANES), f32),
            pltpu.VMEM((modes * SUBLANES, LANES), f32),
            pltpu.VMEM((rows * SUBLANES, LANES), f32),
        ],
        in_specs=[pl.BlockSpec(memory_space=pltpu.SMEM)] + [pl.BlockSpec(memory_space=pltpu.VMEM)] * 10,
        compiler_params=params(),
        cost_estimate=cost(4),
        name="forward_mix",
    )(place, mixer, gate_in, rates, residue, *carry, gate_out, gain)


def column(row):
    return jnp.transpose(jnp.broadcast_to(row, (SUBLANES, row.shape[1])))[:, 0:1]


def inverse_of(squares, full_width):
    return lax.rsqrt(squares * (1.0 / full_width) + EPS)


def backward_state_kernel(full_width, scaled, mixed, gate_out, stats, rates, final, drive):
    rows, width = mixed.shape
    modes = rates.shape[0] // SUBLANES
    inverse = inverse_of(column(stats[0:1, :]), full_width)
    pull = inverse * inverse * inverse * column(stats[SPAN + 1 : SPAN + 2, :]) * (1.0 / full_width)
    for head in range(width // LANES):
        cut = head_slice(head)
        grad = inverse * scaled[:, cut] - mixed[:, cut] * pull
        to_tokens(drive, head, rows, gate_out[:, cut].astype(f32) * grad)
    zero = jnp.zeros((SUBLANES, LANES), f32)
    state = scan(drive, decays(rates, modes), None, [zero] * modes, rows, None, True)
    for m in range(modes):
        final[m * SUBLANES : (m + 1) * SUBLANES, :] = state[m]


def backward_state(full_width, scaled, mixed, gate_out, stats, rates):
    rows, width = mixed.shape
    return pl.pallas_call(
        functools.partial(backward_state_kernel, full_width),
        out_shape=(
            jax.ShapeDtypeStruct(rates.shape, f32),
            jax.ShapeDtypeStruct((rows * SUBLANES, LANES), f32),
        ),
        compiler_params=params(),
        cost_estimate=cost(2),
        name="backward_state",
    )(scaled, mixed, gate_out, stats, rates)


def backward_mix_kernel(place, drive, rates, residue, start, p1, p2, p3, gate_in, grad, residues, out, carried):
    rows, width = gate_in.shape
    modes = residue.shape[0]
    spread(residue, residues)
    decay = decays(rates, modes)
    res = [tile(residues, m) for m in range(modes)]
    add_planes(place, True, rows, rates, start, (p1, p2, p3), carried)
    scan(drive, decay, res, [tile(carried, m) for m in range(modes)], rows, out, True)
    for head in range(width // LANES):
        cut = head_slice(head)
        grad[:, cut] = (gate_in[:, cut].astype(f32) * from_tokens(out, head, rows)).astype(bf16)


def backward_mix(place, drive, rates, residue, carry, gate_in):
    rows, width = gate_in.shape
    modes = residue.shape[0]
    return pl.pallas_call(
        backward_mix_kernel,
        out_shape=jax.ShapeDtypeStruct((rows, width), bf16),
        scratch_shapes=[
            pltpu.VMEM((modes * SUBLANES, LANES), f32),
            pltpu.VMEM((rows * SUBLANES, LANES), f32),
            pltpu.VMEM((modes * SUBLANES, LANES), f32),
        ],
        in_specs=[pl.BlockSpec(memory_space=pltpu.SMEM)] + [pl.BlockSpec(memory_space=pltpu.VMEM)] * 8,
        compiler_params=params(),
        cost_estimate=cost(4),
        name="backward_mix",
    )(place, drive, rates, residue, *carry, gate_in)


def rows_by_rows(a, b):
    return lax.dot_general(a, b, (((1,), (1,)), ((), ())), preferred_element_type=f32)


def product(a, b):
    return jnp.dot(a, b, preferred_element_type=f32)


def masked(scores, offset, near, transposed):
    if offset == 0:
        rows = lax.broadcasted_iota(jnp.int32, scores.shape, 0)
        columns = lax.broadcasted_iota(jnp.int32, scores.shape, 1)
        allowed = (rows <= columns) if transposed else (columns <= rows)
        return jnp.where(allowed, scores, MASKED)
    return scores + jnp.where(near, 0.0, MASKED)


SCALE = 1.0 / math.sqrt(HEAD_DIM)


def step_heads():
    first = pl.program_id(0) * HEADS_PER_STEP
    return [(first + j, head_slice(j)) for j in range(HEADS_PER_STEP)]


def totals_kernel(place, queries, keys, keys_1, keys_2, totals):
    position = place[0]
    for head, cut in step_heads():
        scores = [
            masked(
                rows_by_rows(block[:, cut], queries[:, cut]) * (SCALE * LOG2E), offset, position >= offset, True
            )
            for offset, block in enumerate((keys, keys_1, keys_2))
        ]
        top = functools.reduce(jnp.maximum, [jnp.max(s, axis=0, keepdims=True) for s in scores])
        total = sum(jnp.sum(jnp.exp2(s - top), axis=0, keepdims=True) for s in scores)
        totals[pl.ds(head, 1), :] = top + jnp.log(total) * LOG2E


def head_block(rows):
    return pl.BlockSpec((rows, GROUP), lambda step, *_: (0, step))


def whole(shape):
    return pl.BlockSpec(shape, lambda head, *_: (0,) * len(shape))


def per_head(kernel, place, operands, specs, out_shape, out_specs, scratch=(), name=None, time=5, vmem=48):
    heads = operands[0].shape[1] // GROUP
    return pl.pallas_call(
        kernel,
        out_shape=out_shape,
        grid_spec=pltpu.PrefetchScalarGridSpec(
            num_scalar_prefetch=1,
            grid=(heads,),
            in_specs=specs,
            out_specs=out_specs,
            scratch_shapes=scratch,
        ),
        compiler_params=params("arbitrary", vmem=vmem),
        cost_estimate=cost(time),
        name=name,
    )(place, *operands)


def row_totals(place, queries, keys, keys_1, keys_2):
    rows, width = queries.shape
    shape = (width // HEAD_DIM, rows)
    block = head_block(rows)
    return per_head(
        totals_kernel,
        place,
        (queries, keys, keys_1, keys_2),
        [block] * 4,
        jax.ShapeDtypeStruct(shape, f32),
        whole(shape),
        name="row_totals",
        time=4,
    )


def value_grads_kernel(
    blocks, place, keys, q0, q1, q2, d0, d1, d2, t0, t1, t2, gain, mixed, s0, s1, s2, scaled, stats, acc
):
    step = pl.program_id(0)
    position = place[0]

    @pl.when(step == 0)
    def _():
        acc[...] = jnp.zeros_like(acc)

    for head, cut in step_heads():
        grad = None
        for offset, (query, cotangent, total) in enumerate(((q0, d0, t0), (q1, d1, t1), (q2, d2, t2))):
            scores = rows_by_rows(keys[:, cut], query[:, cut]) * (SCALE * LOG2E)
            scores = masked(scores, offset, position + offset < blocks, True)
            probs = jnp.exp2(scores - total[pl.ds(head, 1), :])
            part = product(probs.astype(bf16), cotangent[:, cut])
            grad = part if grad is None else grad + part
        value = grad * gain[:, cut]
        scaled[:, cut] = value
        acc[...] += value * mixed[:, cut]

    @pl.when(step == pl.num_programs(0) - 1)
    def _():
        for i, squares in enumerate((s0, s1, s2)):
            stats[i : i + 1, :] = squares[...]
        stats[SPAN + 1 : SPAN + 2, :] = row_total(acc[...])


def value_grads(blocks, place, keys, queries, cotangents, totals, gain, mixed, squares):
    rows, width = keys.shape
    heads = width // HEAD_DIM
    block = head_block(rows)
    stat = whole((heads, rows))
    return per_head(
        functools.partial(value_grads_kernel, blocks),
        place,
        (keys, *queries, *cotangents, *totals, gain, mixed, *squares),
        [block] * 7 + [stat] * 3 + [head_block(1), block] + [whole((1, rows))] * 3,
        (jax.ShapeDtypeStruct((rows, width), f32), jax.ShapeDtypeStruct((SPAN + 2, rows), f32)),
        (block, whole((SPAN + 2, rows))),
        scratch=[pltpu.VMEM((rows, LANES), f32)],
        name="value_grads",
        time=7,
    )


def attend_kernel(
    full_width, place, queries, cotangent, k0, k1, k2, v0, v1, v2, stats, totals, attended, grad, delta, columns
):
    position = place[0]

    @pl.when(pl.program_id(0) == 0)
    def _():
        columns[...] = jnp.transpose(totals[...])

    lane = lax.broadcasted_iota(jnp.int32, columns.shape, 1)
    inverses = [inverse_of(stats[i : i + 1, :], full_width) for i in range(SPAN + 1)]
    for head, cut in step_heads():
        log_total = jnp.sum(jnp.where(lane == head, columns[...], 0.0), axis=1, keepdims=True)
        probs = []
        output = None
        for offset, (key, value) in enumerate(((k0, v0), (k1, v1), (k2, v2))):
            scores = rows_by_rows(queries[:, cut], key[:, cut]) * (SCALE * LOG2E)
            scores = masked(scores, offset, position >= offset, False)
            prob = jnp.exp2(scores - log_total)
            probs.append(prob)
            part = product((prob * inverses[offset]).astype(bf16), value[:, cut])
            output = part if output is None else output + part
        result = output.astype(bf16)
        attended[:, cut] = result
        weighed = cotangent[:, cut].astype(f32) * result.astype(f32)
        delta[pl.ds(head, 1), :] = row_total(weighed)
        delta_column = jnp.sum(weighed, axis=1, keepdims=True)
        total = None
        for prob, inverse, key, value in zip(probs, inverses, (k0, k1, k2), (v0, v1, v2)):
            dprob = rows_by_rows(cotangent[:, cut], value[:, cut]) * inverse
            dscore = (prob * (dprob - delta_column)).astype(bf16)
            part = product(dscore, key[:, cut])
            total = part if total is None else total + part
        grad[:, cut] = (total * SCALE).astype(bf16)


def attend(full_width, place, queries, cotangent, keys, values, stats, totals):
    rows, width = queries.shape
    heads = width // HEAD_DIM
    block = head_block(rows)
    stat = whole((heads, rows))
    out = jax.ShapeDtypeStruct((rows, width), bf16)
    return per_head(
        functools.partial(attend_kernel, full_width),
        place,
        (queries, cotangent, *keys, *values, stats, totals),
        [block] * 8 + [whole((SPAN + 2, rows)), stat],
        (out, out, jax.ShapeDtypeStruct((heads, rows), f32)),
        (block, block, stat),
        scratch=[pltpu.VMEM((rows, heads), f32)],
        name="attend",
        vmem=61,
        time=10,
    )


def key_grads_kernel(
    full_width, blocks, place, keys, values, q0, q1, q2, d0, d1, d2, t0, t1, t2, e0, e1, e2, squares, grad
):
    position = place[0]
    inverse = inverse_of(column(squares[0:1, :]), full_width)
    groups = ((q0, d0, t0, e0), (q1, d1, t1, e1), (q2, d2, t2, e2))
    for head, cut in step_heads():
        total = None
        for offset, (query, cotangent, log_total, delta) in enumerate(groups):
            scores = rows_by_rows(keys[:, cut], query[:, cut]) * (SCALE * LOG2E)
            scores = masked(scores, offset, position + offset < blocks, True)
            probs = jnp.exp2(scores - log_total[pl.ds(head, 1), :])
            dprob = rows_by_rows(values[:, cut], cotangent[:, cut]) * inverse
            dscore = (probs * (dprob - delta[pl.ds(head, 1), :])).astype(bf16)
            part = product(dscore, query[:, cut])
            total = part if total is None else total + part
        grad[:, cut] = (total * SCALE).astype(bf16)


def key_grads(full_width, blocks, place, keys, values, queries, cotangents, totals, deltas, squares):
    rows, width = keys.shape
    heads = width // HEAD_DIM
    block = head_block(rows)
    stat = whole((heads, rows))
    return per_head(
        functools.partial(key_grads_kernel, full_width, blocks),
        place,
        (keys, values, *queries, *cotangents, *totals, *deltas, squares),
        [block] * 8 + [stat] * 6 + [whole((SPAN + 2, rows))],
        jax.ShapeDtypeStruct((rows, width), bf16),
        block,
        name="key_grads",
        time=8,
    )


def shards(
    mixer_input, gate_in, gate_out, residue, decay_rate, norm_gain, queries, key_vectors, grad_out
):
    length, width = queries.shape
    full_width = width * lax.axis_size("tp")
    blocks = lax.axis_size("ctx")
    place = lax.axis_index("ctx").reshape(1).astype(jnp.int32)
    gain = norm_gain[None, :]
    residue = jnp.transpose(residue)

    keys_1 = shifted(key_vectors, 1)
    keys_2 = shifted(keys_1, 1)
    queries_1 = shifted(queries, -1)
    cotangent_1 = shifted(grad_out, -1)
    queries_2 = shifted(queries_1, -1)
    cotangent_2 = shifted(cotangent_1, -1)

    final, rates = forward_state(mixer_input, gate_in, jnp.transpose(decay_rate))
    carry = carry_in(final, rates, length, False)
    mixed, scaled_mix, squares = forward_mix(
        place, mixer_input, gate_in, rates, residue, carry, gate_out, gain
    )
    mix_1 = shifted(scaled_mix, 1)
    mix_2 = shifted(mix_1, 1)

    all_squares = (squares, shifted(squares, 1), shifted(squares, 2))
    totals = row_totals(place, queries, key_vectors, keys_1, keys_2)
    totals_1 = shifted(totals, -1)
    totals_2 = shifted(totals, -2)
    all_queries = (queries, queries_1, queries_2)
    all_cotangents = (grad_out, cotangent_1, cotangent_2)
    all_totals = (totals, totals_1, totals_2)
    scaled, stats = value_grads(
        blocks, place, key_vectors, all_queries, all_cotangents, all_totals, gain, mixed, all_squares
    )
    stats = lax.psum(stats, "tp")
    final, drive = backward_state(full_width, scaled, mixed, gate_out, stats, rates)
    carry = carry_in(final, rates, length, True)
    grad_input = backward_mix(place, drive, rates, residue, carry, gate_in)

    attended, grad_queries, delta = attend(
        full_width,
        place,
        queries,
        grad_out,
        (key_vectors, keys_1, keys_2),
        (scaled_mix, mix_1, mix_2),
        stats,
        totals,
    )
    all_deltas = (delta, shifted(delta, -1), shifted(delta, -2))
    grad_keys = key_grads(
        full_width,
        blocks,
        place,
        key_vectors,
        scaled_mix,
        all_queries,
        all_cotangents,
        all_totals,
        all_deltas,
        stats,
    )
    return (attended, grad_queries, grad_keys, grad_input)


def solution(mesh):
    in_specs = (
        P("ctx", "tp"),
        P("ctx", "tp"),
        P("ctx", "tp"),
        P("tp", None),
        P("tp", None),
        P("tp"),
        P("ctx", "tp"),
        P("ctx", "tp"),
        P("ctx", "tp"),
    )
    out_specs = (P("ctx", "tp"), P("ctx", "tp"), P("ctx", "tp"), P("ctx", "tp"))
    return jax.shard_map(shards, mesh=mesh, in_specs=in_specs, out_specs=out_specs, check_vma=False)
```

```python
import functools
import math

import jax
import jax.numpy as jnp
from jax import lax
from jax.experimental import pallas as pl
from jax.experimental.pallas import tpu as pltpu
from jax.sharding import PartitionSpec as P

HEAD_DIM = 128
SPAN = 2
EPS = 1e-06
LOG2E = 1.4426950408889634
MASKED = -1e30
LANES = 128
SUBLANES = 8
ROWS_PER_STEP = 8
HEADS_PER_STEP = 4
GROUP = HEADS_PER_STEP * HEAD_DIM
f32 = jnp.float32
bf16 = jnp.bfloat16


COST = 0.3


def cost(microseconds):
    microseconds = microseconds * COST
    return pl.CostEstimate(
        flops=int(microseconds * 1.0e9), bytes_accessed=int(microseconds * 2.0e6), transcendentals=0
    )


def params(*semantics, vmem=48):
    return pltpu.CompilerParams(dimension_semantics=semantics or None, vmem_limit_bytes=vmem << 20)


def shifted(value, by):
    devices = lax.axis_size("ctx")
    return lax.ppermute(value, "ctx", [(i, (i + by) % devices) for i in range(devices)])


def along(value, axis, by):
    def target(i):
        place = [i // 8, (i // 4) % 2, i % 4]
        size = (4, 2, 4)
        place[axis] = (place[axis] + by) % size[axis]
        return (place[0] * 2 + place[1]) * 4 + place[2]

    return lax.ppermute(value, "ctx", [(i, target(i)) for i in range(32)])


def after(value, *others):
    return lax.optimization_barrier((value, *others))[0]


def carry_in(final, rate, length, reverse):
    position = lax.axis_index("ctx")
    position = (31 - position) if reverse else position
    sign = -1 if reverse else 1
    x, y, z = position // 8, (position // 4) % 2, position % 4

    def decayed(blocks, keep=True):
        blocks = jnp.asarray(blocks, f32)
        return jnp.where(keep, jnp.exp(-rate * (length * jnp.maximum(blocks, 0.0))), 0.0)

    others = [along(final, 2, sign * d) for d in (1, 2, 3)]
    state = sum(decayed(d - 1, d <= z) * other for d, other in zip((1, 2, 3), others))
    group = decayed(3 - z) * final
    for d, other in zip((1, 2, 3), others):
        group = group + decayed(3 - (z - d) % 4) * other
    partner = along(group, 1, 1)
    state = state + decayed(z, y == 1) * partner
    pair = jnp.where(y == 1, group + decayed(4) * partner, partner + decayed(4) * group)
    planes = [along(pair, 0, sign * d) for d in (1, 2, 3)]
    return (state, *planes)


def add_planes(place, reverse, length, rates, start, planes, target):
    position = (31 - place[0]) if reverse else place[0]
    state = start[...]
    for d, plane in zip((1, 2, 3), planes):
        blocks = (position % 8 + 8 * (d - 1)).astype(f32)
        factor = jnp.exp(-rates[...] * (blocks * length))
        state = state + plane[...] * jnp.where(position >= 8 * d, factor, 0.0)
    target[...] = state


def to_tokens(scratch, head, rows, block):
    scratch[pl.ds(head, rows, SUBLANES), :] = block


def from_tokens(scratch, head, rows):
    return scratch[pl.ds(head, rows, SUBLANES), :]


def head_slice(head):
    return slice(head * LANES, (head + 1) * LANES)


def tile(ref, m):
    return ref[m * SUBLANES : (m + 1) * SUBLANES, :]


def scan(drive, decay, residue, state, rows, out, reverse):
    modes = len(decay)

    def step(i, state):
        state = list(state)
        for j in range(ROWS_PER_STEP):
            t = i * ROWS_PER_STEP + j
            t = (rows - 1 - t) if reverse else t
            place = pl.ds(pl.multiple_of(t * SUBLANES, SUBLANES), SUBLANES)
            row = drive[place, :]
            state = [decay[m] * state[m] + row for m in range(modes)]
            if out is not None:
                terms = [residue[m] * state[m] for m in range(modes)]
                while len(terms) > 1:
                    terms = [a + b for a, b in zip(terms[::2], terms[1::2])]
                out[place, :] = terms[0]
        return tuple(state)

    return lax.fori_loop(0, rows // ROWS_PER_STEP, step, tuple(state))


def spread(source, target):
    modes, width = source.shape
    for head in range(width // LANES):
        to_tokens(target, head, modes, source[:, head_slice(head)])


def decays(rates, modes):
    return [jnp.exp(-tile(rates, m)) for m in range(modes)]


def form_drive(mixer, gate_in, drive):
    rows, width = mixer.shape
    for head in range(width // LANES):
        cut = head_slice(head)
        to_tokens(drive, head, rows, mixer[:, cut].astype(f32) * gate_in[:, cut].astype(f32))


def forward_state_kernel(mixer, gate_in, rate, final, rates, drive):
    rows, width = mixer.shape
    modes = rate.shape[0]
    spread(rate, rates)
    form_drive(mixer, gate_in, drive)
    zero = jnp.zeros((SUBLANES, LANES), f32)
    state = scan(drive, decays(rates, modes), None, [zero] * modes, rows, None, False)
    for m in range(modes):
        final[m * SUBLANES : (m + 1) * SUBLANES, :] = state[m]


def forward_state(mixer, gate_in, rate):
    rows, width = mixer.shape
    modes = rate.shape[0]
    small = jax.ShapeDtypeStruct((modes * SUBLANES, LANES), f32)
    return pl.pallas_call(
        forward_state_kernel,
        out_shape=(small, small),
        scratch_shapes=[pltpu.VMEM((rows * SUBLANES, LANES), f32)],
        compiler_params=params(),
        cost_estimate=cost(2),
        name="forward_state",
    )(mixer, gate_in, rate)


def row_total(block):
    ones = jnp.ones((SUBLANES, LANES), f32)
    totals = lax.dot_general(
        ones, block, (((1,), (1,)), ((), ())), precision=lax.Precision.HIGHEST, preferred_element_type=f32
    )
    return totals[0:1, :]


def forward_mix_kernel(
    place,
    mixer,
    gate_in,
    rates,
    residue,
    start,
    p1,
    p2,
    p3,
    gate_out,
    gain,
    mixed,
    scaled,
    squares,
    residues,
    out,
    carried,
    drive,
):
    rows, width = mixed.shape
    modes = residue.shape[0]
    spread(residue, residues)
    decay = decays(rates, modes)
    res = [tile(residues, m) for m in range(modes)]
    form_drive(mixer, gate_in, drive)
    add_planes(place, False, rows, rates, start, (p1, p2, p3), carried)
    scan(drive, decay, res, [tile(carried, m) for m in range(modes)], rows, out, False)
    total = jnp.zeros((rows, LANES), f32)
    for head in range(width // LANES):
        cut = head_slice(head)
        value = gate_out[:, cut].astype(f32) * from_tokens(out, head, rows)
        mixed[:, cut] = value
        scaled[:, cut] = (value * gain[:, cut]).astype(bf16)
        total = total + value * value
    squares[...] = row_total(total)


def forward_mix(place, mixer, gate_in, rates, residue, carry, gate_out, gain):
    rows, width = gate_out.shape
    modes = residue.shape[0]
    return pl.pallas_call(
        forward_mix_kernel,
        out_shape=(
            jax.ShapeDtypeStruct((rows, width), f32),
            jax.ShapeDtypeStruct((rows, width), bf16),
            jax.ShapeDtypeStruct((1, rows), f32),
        ),
        scratch_shapes=[
            pltpu.VMEM((modes * SUBLANES, LANES), f32),
            pltpu.VMEM((rows * SUBLANES, LANES), f32),
            pltpu.VMEM((modes * SUBLANES, LANES), f32),
            pltpu.VMEM((rows * SUBLANES, LANES), f32),
        ],
        in_specs=[pl.BlockSpec(memory_space=pltpu.SMEM)] + [pl.BlockSpec(memory_space=pltpu.VMEM)] * 10,
        compiler_params=params(),
        cost_estimate=cost(4),
        name="forward_mix",
    )(place, mixer, gate_in, rates, residue, *carry, gate_out, gain)


def column(row):
    return jnp.transpose(jnp.broadcast_to(row, (SUBLANES, row.shape[1])))[:, 0:1]


def inverse_of(squares, full_width):
    return lax.rsqrt(squares * (1.0 / full_width) + EPS)


def backward_state_kernel(full_width, scaled, mixed, gate_out, stats, rates, final, drive):
    rows, width = mixed.shape
    modes = rates.shape[0] // SUBLANES
    inverse = inverse_of(column(stats[0:1, :]), full_width)
    pull = inverse * inverse * inverse * column(stats[SPAN + 1 : SPAN + 2, :]) * (1.0 / full_width)
    for head in range(width // LANES):
        cut = head_slice(head)
        grad = inverse * scaled[:, cut] - mixed[:, cut] * pull
        to_tokens(drive, head, rows, gate_out[:, cut].astype(f32) * grad)
    zero = jnp.zeros((SUBLANES, LANES), f32)
    state = scan(drive, decays(rates, modes), None, [zero] * modes, rows, None, True)
    for m in range(modes):
        final[m * SUBLANES : (m + 1) * SUBLANES, :] = state[m]


def backward_state(full_width, scaled, mixed, gate_out, stats, rates):
    rows, width = mixed.shape
    return pl.pallas_call(
        functools.partial(backward_state_kernel, full_width),
        out_shape=(
            jax.ShapeDtypeStruct(rates.shape, f32),
            jax.ShapeDtypeStruct((rows * SUBLANES, LANES), f32),
        ),
        compiler_params=params(),
        cost_estimate=cost(2),
        name="backward_state",
    )(scaled, mixed, gate_out, stats, rates)


def backward_mix_kernel(place, drive, rates, residue, start, p1, p2, p3, gate_in, grad, residues, out, carried):
    rows, width = gate_in.shape
    modes = residue.shape[0]
    spread(residue, residues)
    decay = decays(rates, modes)
    res = [tile(residues, m) for m in range(modes)]
    add_planes(place, True, rows, rates, start, (p1, p2, p3), carried)
    scan(drive, decay, res, [tile(carried, m) for m in range(modes)], rows, out, True)
    for head in range(width // LANES):
        cut = head_slice(head)
        grad[:, cut] = (gate_in[:, cut].astype(f32) * from_tokens(out, head, rows)).astype(bf16)


def backward_mix(place, drive, rates, residue, carry, gate_in):
    rows, width = gate_in.shape
    modes = residue.shape[0]
    return pl.pallas_call(
        backward_mix_kernel,
        out_shape=jax.ShapeDtypeStruct((rows, width), bf16),
        scratch_shapes=[
            pltpu.VMEM((modes * SUBLANES, LANES), f32),
            pltpu.VMEM((rows * SUBLANES, LANES), f32),
            pltpu.VMEM((modes * SUBLANES, LANES), f32),
        ],
        in_specs=[pl.BlockSpec(memory_space=pltpu.SMEM)] + [pl.BlockSpec(memory_space=pltpu.VMEM)] * 8,
        compiler_params=params(),
        cost_estimate=cost(4),
        name="backward_mix",
    )(place, drive, rates, residue, *carry, gate_in)


def rows_by_rows(a, b):
    return lax.dot_general(a, b, (((1,), (1,)), ((), ())), preferred_element_type=f32)


def product(a, b):
    return jnp.dot(a, b, preferred_element_type=f32)


def masked(scores, offset, near, transposed):
    if offset == 0:
        rows = lax.broadcasted_iota(jnp.int32, scores.shape, 0)
        columns = lax.broadcasted_iota(jnp.int32, scores.shape, 1)
        allowed = (rows <= columns) if transposed else (columns <= rows)
        return jnp.where(allowed, scores, MASKED)
    return scores + jnp.where(near, 0.0, MASKED)


SCALE = 1.0 / math.sqrt(HEAD_DIM)


def step_heads():
    first = pl.program_id(0) * HEADS_PER_STEP
    return [(first + j, head_slice(j)) for j in range(HEADS_PER_STEP)]


def totals_kernel(place, queries, keys, keys_1, keys_2, totals):
    position = place[0]
    for head, cut in step_heads():
        scores = [
            masked(
                rows_by_rows(block[:, cut], queries[:, cut]) * (SCALE * LOG2E), offset, position >= offset, True
            )
            for offset, block in enumerate((keys, keys_1, keys_2))
        ]
        top = functools.reduce(jnp.maximum, [jnp.max(s, axis=0, keepdims=True) for s in scores])
        total = sum(jnp.sum(jnp.exp2(s - top), axis=0, keepdims=True) for s in scores)
        totals[pl.ds(head, 1), :] = top + jnp.log(total) * LOG2E


def head_block(rows):
    return pl.BlockSpec((rows, GROUP), lambda step, *_: (0, step))


def whole(shape):
    return pl.BlockSpec(shape, lambda head, *_: (0,) * len(shape))


def per_head(kernel, place, operands, specs, out_shape, out_specs, scratch=(), name=None, time=5, vmem=48):
    heads = operands[0].shape[1] // GROUP
    return pl.pallas_call(
        kernel,
        out_shape=out_shape,
        grid_spec=pltpu.PrefetchScalarGridSpec(
            num_scalar_prefetch=1,
            grid=(heads,),
            in_specs=specs,
            out_specs=out_specs,
            scratch_shapes=scratch,
        ),
        compiler_params=params("arbitrary", vmem=vmem),
        cost_estimate=cost(time),
        name=name,
    )(place, *operands)


def row_totals(place, queries, keys, keys_1, keys_2):
    rows, width = queries.shape
    shape = (width // HEAD_DIM, rows)
    block = head_block(rows)
    return per_head(
        totals_kernel,
        place,
        (queries, keys, keys_1, keys_2),
        [block] * 4,
        jax.ShapeDtypeStruct(shape, f32),
        whole(shape),
        name="row_totals",
        time=4,
    )


def value_grads_kernel(
    blocks, place, keys, q0, q1, q2, d0, d1, d2, t0, t1, t2, gain, mixed, s0, s1, s2, scaled, stats, acc
):
    step = pl.program_id(0)
    position = place[0]

    @pl.when(step == 0)
    def _():
        acc[...] = jnp.zeros_like(acc)

    for head, cut in step_heads():
        grad = None
        for offset, (query, cotangent, total) in enumerate(((q0, d0, t0), (q1, d1, t1), (q2, d2, t2))):
            scores = rows_by_rows(keys[:, cut], query[:, cut]) * (SCALE * LOG2E)
            scores = masked(scores, offset, position + offset < blocks, True)
            probs = jnp.exp2(scores - total[pl.ds(head, 1), :])
            part = product(probs.astype(bf16), cotangent[:, cut])
            grad = part if grad is None else grad + part
        value = grad * gain[:, cut]
        scaled[:, cut] = value
        acc[...] += value * mixed[:, cut]

    @pl.when(step == pl.num_programs(0) - 1)
    def _():
        for i, squares in enumerate((s0, s1, s2)):
            stats[i : i + 1, :] = squares[...]
        stats[SPAN + 1 : SPAN + 2, :] = row_total(acc[...])


def value_grads(blocks, place, keys, queries, cotangents, totals, gain, mixed, squares):
    rows, width = keys.shape
    heads = width // HEAD_DIM
    block = head_block(rows)
    stat = whole((heads, rows))
    return per_head(
        functools.partial(value_grads_kernel, blocks),
        place,
        (keys, *queries, *cotangents, *totals, gain, mixed, *squares),
        [block] * 7 + [stat] * 3 + [head_block(1), block] + [whole((1, rows))] * 3,
        (jax.ShapeDtypeStruct((rows, width), f32), jax.ShapeDtypeStruct((SPAN + 2, rows), f32)),
        (block, whole((SPAN + 2, rows))),
        scratch=[pltpu.VMEM((rows, LANES), f32)],
        name="value_grads",
        time=7,
    )


def attend_kernel(
    full_width, place, queries, cotangent, k0, k1, k2, v0, v1, v2, stats, totals, attended, grad, delta, columns
):
    position = place[0]

    @pl.when(pl.program_id(0) == 0)
    def _():
        columns[...] = jnp.transpose(totals[...])

    lane = lax.broadcasted_iota(jnp.int32, columns.shape, 1)
    inverses = [inverse_of(stats[i : i + 1, :], full_width) for i in range(SPAN + 1)]
    for head, cut in step_heads():
        log_total = jnp.sum(jnp.where(lane == head, columns[...], 0.0), axis=1, keepdims=True)
        probs = []
        output = None
        for offset, (key, value) in enumerate(((k0, v0), (k1, v1), (k2, v2))):
            scores = rows_by_rows(queries[:, cut], key[:, cut]) * (SCALE * LOG2E)
            scores = masked(scores, offset, position >= offset, False)
            prob = jnp.exp2(scores - log_total)
            probs.append(prob)
            part = product((prob * inverses[offset]).astype(bf16), value[:, cut])
            output = part if output is None else output + part
        result = output.astype(bf16)
        attended[:, cut] = result
        weighed = cotangent[:, cut].astype(f32) * result.astype(f32)
        delta[pl.ds(head, 1), :] = row_total(weighed)
        delta_column = jnp.sum(weighed, axis=1, keepdims=True)
        total = None
        for prob, inverse, key, value in zip(probs, inverses, (k0, k1, k2), (v0, v1, v2)):
            dprob = rows_by_rows(cotangent[:, cut], value[:, cut]) * inverse
            dscore = (prob * (dprob - delta_column)).astype(bf16)
            part = product(dscore, key[:, cut])
            total = part if total is None else total + part
        grad[:, cut] = (total * SCALE).astype(bf16)


def attend(full_width, place, queries, cotangent, keys, values, stats, totals):
    rows, width = queries.shape
    heads = width // HEAD_DIM
    block = head_block(rows)
    stat = whole((heads, rows))
    out = jax.ShapeDtypeStruct((rows, width), bf16)
    return per_head(
        functools.partial(attend_kernel, full_width),
        place,
        (queries, cotangent, *keys, *values, stats, totals),
        [block] * 8 + [whole((SPAN + 2, rows)), stat],
        (out, out, jax.ShapeDtypeStruct((heads, rows), f32)),
        (block, block, stat),
        scratch=[pltpu.VMEM((rows, heads), f32)],
        name="attend",
        vmem=61,
        time=10,
    )


def key_grads_kernel(
    full_width, blocks, place, keys, values, q0, q1, q2, d0, d1, d2, t0, t1, t2, e0, e1, e2, squares, grad
):
    position = place[0]
    inverse = inverse_of(column(squares[0:1, :]), full_width)
    groups = ((q0, d0, t0, e0), (q1, d1, t1, e1), (q2, d2, t2, e2))
    for head, cut in step_heads():
        total = None
        for offset, (query, cotangent, log_total, delta) in enumerate(groups):
            scores = rows_by_rows(keys[:, cut], query[:, cut]) * (SCALE * LOG2E)
            scores = masked(scores, offset, position + offset < blocks, True)
            probs = jnp.exp2(scores - log_total[pl.ds(head, 1), :])
            dprob = rows_by_rows(values[:, cut], cotangent[:, cut]) * inverse
            dscore = (probs * (dprob - delta[pl.ds(head, 1), :])).astype(bf16)
            part = product(dscore, query[:, cut])
            total = part if total is None else total + part
        grad[:, cut] = (total * SCALE).astype(bf16)


def key_grads(full_width, blocks, place, keys, values, queries, cotangents, totals, deltas, squares):
    rows, width = keys.shape
    heads = width // HEAD_DIM
    block = head_block(rows)
    stat = whole((heads, rows))
    return per_head(
        functools.partial(key_grads_kernel, full_width, blocks),
        place,
        (keys, values, *queries, *cotangents, *totals, *deltas, squares),
        [block] * 8 + [stat] * 6 + [whole((SPAN + 2, rows))],
        jax.ShapeDtypeStruct((rows, width), bf16),
        block,
        name="key_grads",
        time=8,
    )


def shards(
    mixer_input, gate_in, gate_out, residue, decay_rate, norm_gain, queries, key_vectors, grad_out
):
    length, width = queries.shape
    full_width = width * lax.axis_size("tp")
    blocks = lax.axis_size("ctx")
    place = lax.axis_index("ctx").reshape(1).astype(jnp.int32)
    gain = norm_gain[None, :]
    residue = jnp.transpose(residue)

    keys_1 = shifted(key_vectors, 1)
    keys_2 = shifted(keys_1, 1)
    queries_1 = shifted(queries, -1)
    cotangent_1 = shifted(grad_out, -1)
    queries_2 = shifted(queries_1, -1)
    cotangent_2 = shifted(cotangent_1, -1)

    final, rates = forward_state(mixer_input, gate_in, jnp.transpose(decay_rate))
    carry = carry_in(final, rates, length, False)
    mixed, scaled_mix, squares = forward_mix(
        place, mixer_input, gate_in, rates, residue, carry, gate_out, gain
    )
    mix_1 = shifted(scaled_mix, 1)
    mix_2 = shifted(mix_1, 1)

    totals = row_totals(place, queries, key_vectors, keys_1, keys_2)
    totals_1 = shifted(totals, -1)
    totals_2 = shifted(totals, -2)
    late = after(squares, totals)
    all_squares = (squares, shifted(late, 1), shifted(late, 2))
    all_queries = (queries, queries_1, queries_2)
    all_cotangents = (grad_out, cotangent_1, cotangent_2)
    all_totals = (totals, totals_1, totals_2)
    scaled, stats = value_grads(
        blocks, place, key_vectors, all_queries, all_cotangents, all_totals, gain, mixed, all_squares
    )
    stats = lax.psum(stats, "tp")
    final, drive = backward_state(full_width, scaled, mixed, gate_out, stats, rates)
    carry = carry_in(final, rates, length, True)
    grad_input = backward_mix(place, drive, rates, residue, carry, gate_in)

    attended, grad_queries, delta = attend(
        full_width,
        place,
        queries,
        grad_out,
        (key_vectors, keys_1, keys_2),
        (scaled_mix, mix_1, mix_2),
        stats,
        totals,
    )
    all_deltas = (delta, shifted(delta, -1), shifted(delta, -2))
    grad_keys = key_grads(
        full_width,
        blocks,
        place,
        key_vectors,
        scaled_mix,
        all_queries,
        all_cotangents,
        all_totals,
        all_deltas,
        stats,
    )
    return (attended, grad_queries, grad_keys, grad_input)


def solution(mesh):
    in_specs = (
        P("ctx", "tp"),
        P("ctx", "tp"),
        P("ctx", "tp"),
        P("tp", None),
        P("tp", None),
        P("tp"),
        P("ctx", "tp"),
        P("ctx", "tp"),
        P("ctx", "tp"),
    )
    out_specs = (P("ctx", "tp"), P("ctx", "tp"), P("ctx", "tp"), P("ctx", "tp"))
    return jax.shard_map(shards, mesh=mesh, in_specs=in_specs, out_specs=out_specs, check_vma=False)
```

```python
import functools
import math

import jax
import jax.numpy as jnp
from jax import lax
from jax.experimental import pallas as pl
from jax.experimental.pallas import tpu as pltpu
from jax.sharding import PartitionSpec as P

HEAD_DIM = 128
SPAN = 2
EPS = 1e-06
LOG2E = 1.4426950408889634
MASKED = -1e30
LANES = 128
SUBLANES = 8
ROWS_PER_STEP = 16
GROUP = 4 * HEAD_DIM
f32 = jnp.float32
bf16 = jnp.bfloat16


COST = 0.3


def cost(microseconds):
    microseconds = microseconds * COST
    return pl.CostEstimate(
        flops=int(microseconds * 1.0e9), bytes_accessed=int(microseconds * 2.0e6), transcendentals=0
    )


def params(*semantics, vmem=48):
    return pltpu.CompilerParams(dimension_semantics=semantics or None, vmem_limit_bytes=vmem << 20)


def shifted(value, by):
    devices = lax.axis_size("ctx")
    return lax.ppermute(value, "ctx", [(i, (i + by) % devices) for i in range(devices)])


def along(value, axis, by):
    def target(i):
        place = [i // 8, (i // 4) % 2, i % 4]
        size = (4, 2, 4)
        place[axis] = (place[axis] + by) % size[axis]
        return (place[0] * 2 + place[1]) * 4 + place[2]

    return lax.ppermute(value, "ctx", [(i, target(i)) for i in range(32)])


def after(value, *others):
    return lax.optimization_barrier((value, *others))[0]


def carry_in(final, rate, length, reverse):
    position = lax.axis_index("ctx")
    position = (31 - position) if reverse else position
    sign = -1 if reverse else 1
    x, y, z = position // 8, (position // 4) % 2, position % 4

    def decayed(blocks, keep=True):
        blocks = jnp.asarray(blocks, f32)
        return jnp.where(keep, jnp.exp(-rate * (length * jnp.maximum(blocks, 0.0))), 0.0)

    others = [along(final, 2, sign * d) for d in (1, 2, 3)]
    state = sum(decayed(d - 1, d <= z) * other for d, other in zip((1, 2, 3), others))
    group = decayed(3 - z) * final
    for d, other in zip((1, 2, 3), others):
        group = group + decayed(3 - (z - d) % 4) * other
    partner = along(group, 1, 1)
    state = state + decayed(z, y == 1) * partner
    pair = jnp.where(y == 1, group + decayed(4) * partner, partner + decayed(4) * group)
    planes = [along(pair, 0, sign * d) for d in (1, 2, 3)]
    return (state, *planes)


def add_planes(place, reverse, length, rates, start, planes, target):
    position = (31 - place[0]) if reverse else place[0]
    state = start[...]
    for d, plane in zip((1, 2, 3), planes):
        blocks = (position % 8 + 8 * (d - 1)).astype(f32)
        factor = jnp.exp(-rates[...] * (blocks * length))
        state = state + plane[...] * jnp.where(position >= 8 * d, factor, 0.0)
    target[...] = state


def to_tokens(scratch, head, rows, block):
    scratch[pl.ds(head, rows, SUBLANES), :] = block


def from_tokens(scratch, head, rows):
    return scratch[pl.ds(head, rows, SUBLANES), :]


def head_slice(head):
    return slice(head * LANES, (head + 1) * LANES)


def tile(ref, m):
    return ref[m * SUBLANES : (m + 1) * SUBLANES, :]


def scan(drive, decay, residue, state, rows, out, reverse):
    modes = len(decay)

    def step(i, state):
        state = list(state)
        for j in range(ROWS_PER_STEP):
            t = i * ROWS_PER_STEP + j
            t = (rows - 1 - t) if reverse else t
            place = pl.ds(pl.multiple_of(t * SUBLANES, SUBLANES), SUBLANES)
            row = drive[place, :]
            state = [decay[m] * state[m] + row for m in range(modes)]
            if out is not None:
                terms = [residue[m] * state[m] for m in range(modes)]
                while len(terms) > 1:
                    terms = [a + b for a, b in zip(terms[::2], terms[1::2])]
                out[place, :] = terms[0]
        return tuple(state)

    return lax.fori_loop(0, rows // ROWS_PER_STEP, step, tuple(state))


def spread(source, target):
    modes, width = source.shape
    for head in range(width // LANES):
        to_tokens(target, head, modes, source[:, head_slice(head)])


def decays(rates, modes):
    return [jnp.exp(-tile(rates, m)) for m in range(modes)]


def form_drive(mixer, gate_in, drive):
    rows, width = mixer.shape
    for head in range(width // LANES):
        cut = head_slice(head)
        to_tokens(drive, head, rows, mixer[:, cut].astype(f32) * gate_in[:, cut].astype(f32))


def forward_state_kernel(mixer, gate_in, rate, final, rates, drive):
    rows, width = mixer.shape
    modes = rate.shape[0]
    spread(rate, rates)
    form_drive(mixer, gate_in, drive)
    zero = jnp.zeros((SUBLANES, LANES), f32)
    state = scan(drive, decays(rates, modes), None, [zero] * modes, rows, None, False)
    for m in range(modes):
        final[m * SUBLANES : (m + 1) * SUBLANES, :] = state[m]


def forward_state(mixer, gate_in, rate):
    rows, width = mixer.shape
    modes = rate.shape[0]
    small = jax.ShapeDtypeStruct((modes * SUBLANES, LANES), f32)
    return pl.pallas_call(
        forward_state_kernel,
        out_shape=(small, small),
        scratch_shapes=[pltpu.VMEM((rows * SUBLANES, LANES), f32)],
        compiler_params=params(),
        cost_estimate=cost(2),
        name="forward_state",
    )(mixer, gate_in, rate)


def row_total(block):
    ones = jnp.ones((SUBLANES, LANES), f32)
    totals = lax.dot_general(
        ones, block, (((1,), (1,)), ((), ())), precision=lax.Precision.HIGHEST, preferred_element_type=f32
    )
    return totals[0:1, :]


def forward_mix_kernel(
    place,
    mixer,
    gate_in,
    rates,
    residue,
    start,
    p1,
    p2,
    p3,
    gate_out,
    gain,
    mixed,
    scaled,
    squares,
    residues,
    out,
    carried,
    drive,
):
    rows, width = mixed.shape
    modes = residue.shape[0]
    spread(residue, residues)
    decay = decays(rates, modes)
    res = [tile(residues, m) for m in range(modes)]
    form_drive(mixer, gate_in, drive)
    add_planes(place, False, rows, rates, start, (p1, p2, p3), carried)
    scan(drive, decay, res, [tile(carried, m) for m in range(modes)], rows, out, False)
    total = jnp.zeros((rows, LANES), f32)
    for head in range(width // LANES):
        cut = head_slice(head)
        value = gate_out[:, cut].astype(f32) * from_tokens(out, head, rows)
        mixed[:, cut] = value
        scaled[:, cut] = (value * gain[:, cut]).astype(bf16)
        total = total + value * value
    squares[...] = row_total(total)


def forward_mix(place, mixer, gate_in, rates, residue, carry, gate_out, gain):
    rows, width = gate_out.shape
    modes = residue.shape[0]
    return pl.pallas_call(
        forward_mix_kernel,
        out_shape=(
            jax.ShapeDtypeStruct((rows, width), f32),
            jax.ShapeDtypeStruct((rows, width), bf16),
            jax.ShapeDtypeStruct((1, rows), f32),
        ),
        scratch_shapes=[
            pltpu.VMEM((modes * SUBLANES, LANES), f32),
            pltpu.VMEM((rows * SUBLANES, LANES), f32),
            pltpu.VMEM((modes * SUBLANES, LANES), f32),
            pltpu.VMEM((rows * SUBLANES, LANES), f32),
        ],
        in_specs=[pl.BlockSpec(memory_space=pltpu.SMEM)] + [pl.BlockSpec(memory_space=pltpu.VMEM)] * 10,
        compiler_params=params(),
        cost_estimate=cost(4),
        name="forward_mix",
    )(place, mixer, gate_in, rates, residue, *carry, gate_out, gain)


def column(row):
    return jnp.transpose(jnp.broadcast_to(row, (SUBLANES, row.shape[1])))[:, 0:1]


def inverse_of(squares, full_width):
    return lax.rsqrt(squares * (1.0 / full_width) + EPS)


def backward_state_kernel(full_width, scaled, mixed, gate_out, stats, rates, final, drive):
    rows, width = mixed.shape
    modes = rates.shape[0] // SUBLANES
    inverse = inverse_of(column(stats[0:1, :]), full_width)
    pull = inverse * inverse * inverse * column(stats[SPAN + 1 : SPAN + 2, :]) * (1.0 / full_width)
    for head in range(width // LANES):
        cut = head_slice(head)
        grad = inverse * scaled[:, cut] - mixed[:, cut] * pull
        to_tokens(drive, head, rows, gate_out[:, cut].astype(f32) * grad)
    zero = jnp.zeros((SUBLANES, LANES), f32)
    state = scan(drive, decays(rates, modes), None, [zero] * modes, rows, None, True)
    for m in range(modes):
        final[m * SUBLANES : (m + 1) * SUBLANES, :] = state[m]


def backward_state(full_width, scaled, mixed, gate_out, stats, rates):
    rows, width = mixed.shape
    return pl.pallas_call(
        functools.partial(backward_state_kernel, full_width),
        out_shape=(
            jax.ShapeDtypeStruct(rates.shape, f32),
            jax.ShapeDtypeStruct((rows * SUBLANES, LANES), f32),
        ),
        compiler_params=params(),
        cost_estimate=cost(2),
        name="backward_state",
    )(scaled, mixed, gate_out, stats, rates)


def backward_mix_kernel(place, drive, rates, residue, start, p1, p2, p3, gate_in, grad, residues, out, carried):
    rows, width = gate_in.shape
    modes = residue.shape[0]
    spread(residue, residues)
    decay = decays(rates, modes)
    res = [tile(residues, m) for m in range(modes)]
    add_planes(place, True, rows, rates, start, (p1, p2, p3), carried)
    scan(drive, decay, res, [tile(carried, m) for m in range(modes)], rows, out, True)
    for head in range(width // LANES):
        cut = head_slice(head)
        grad[:, cut] = (gate_in[:, cut].astype(f32) * from_tokens(out, head, rows)).astype(bf16)


def backward_mix(place, drive, rates, residue, carry, gate_in):
    rows, width = gate_in.shape
    modes = residue.shape[0]
    return pl.pallas_call(
        backward_mix_kernel,
        out_shape=jax.ShapeDtypeStruct((rows, width), bf16),
        scratch_shapes=[
            pltpu.VMEM((modes * SUBLANES, LANES), f32),
            pltpu.VMEM((rows * SUBLANES, LANES), f32),
            pltpu.VMEM((modes * SUBLANES, LANES), f32),
        ],
        in_specs=[pl.BlockSpec(memory_space=pltpu.SMEM)] + [pl.BlockSpec(memory_space=pltpu.VMEM)] * 8,
        compiler_params=params(),
        cost_estimate=cost(4),
        name="backward_mix",
    )(place, drive, rates, residue, *carry, gate_in)


def rows_by_rows(a, b):
    return lax.dot_general(a, b, (((1,), (1,)), ((), ())), preferred_element_type=f32)


def product(a, b):
    return jnp.dot(a, b, preferred_element_type=f32)


def masked(scores, offset, near, transposed):
    if offset == 0:
        rows = lax.broadcasted_iota(jnp.int32, scores.shape, 0)
        columns = lax.broadcasted_iota(jnp.int32, scores.shape, 1)
        allowed = (rows <= columns) if transposed else (columns <= rows)
        return jnp.where(allowed, scores, MASKED)
    return scores + jnp.where(near, 0.0, MASKED)


SCALE = 1.0 / math.sqrt(HEAD_DIM)


def step_heads(block):
    count = block.shape[1] // HEAD_DIM
    first = pl.program_id(0) * count
    return [(first + j, head_slice(j)) for j in range(count)]


def totals_kernel(place, queries, keys, keys_1, keys_2, totals):
    position = place[0]
    for head, cut in step_heads(keys):
        scores = [
            masked(
                rows_by_rows(block[:, cut], queries[:, cut]) * (SCALE * LOG2E), offset, position >= offset, True
            )
            for offset, block in enumerate((keys, keys_1, keys_2))
        ]
        top = functools.reduce(jnp.maximum, [jnp.max(s, axis=0, keepdims=True) for s in scores])
        total = sum(jnp.sum(jnp.exp2(s - top), axis=0, keepdims=True) for s in scores)
        totals[pl.ds(head, 1), :] = top + jnp.log(total) * LOG2E


def head_block(rows, group=GROUP):
    return pl.BlockSpec((rows, group), lambda step, *_: (0, step))


def whole(shape):
    return pl.BlockSpec(shape, lambda head, *_: (0,) * len(shape))


def per_head(kernel, place, operands, specs, out_shape, out_specs, scratch=(), name=None, time=5, vmem=48, group=GROUP):
    steps = operands[0].shape[1] // group
    return pl.pallas_call(
        kernel,
        out_shape=out_shape,
        grid_spec=pltpu.PrefetchScalarGridSpec(
            num_scalar_prefetch=1,
            grid=(steps,),
            in_specs=specs,
            out_specs=out_specs,
            scratch_shapes=scratch,
        ),
        compiler_params=params("arbitrary", vmem=vmem),
        cost_estimate=cost(time),
        name=name,
    )(place, *operands)


def row_totals(place, queries, keys, keys_1, keys_2):
    rows, width = queries.shape
    shape = (width // HEAD_DIM, rows)
    block = head_block(rows, width)
    return per_head(
        totals_kernel,
        place,
        (queries, keys, keys_1, keys_2),
        [block] * 4,
        jax.ShapeDtypeStruct(shape, f32),
        whole(shape),
        name="row_totals",
        group=width,
        time=4,
    )


def value_grads_kernel(
    blocks, place, keys, q0, q1, q2, d0, d1, d2, t0, t1, t2, gain, mixed, s0, s1, s2, scaled, stats, acc
):
    step = pl.program_id(0)
    position = place[0]

    @pl.when(step == 0)
    def _():
        acc[...] = jnp.zeros_like(acc)

    for head, cut in step_heads(keys):
        grad = None
        for offset, (query, cotangent, total) in enumerate(((q0, d0, t0), (q1, d1, t1), (q2, d2, t2))):
            scores = rows_by_rows(keys[:, cut], query[:, cut]) * (SCALE * LOG2E)
            scores = masked(scores, offset, position + offset < blocks, True)
            probs = jnp.exp2(scores - total[pl.ds(head, 1), :])
            part = product(probs.astype(bf16), cotangent[:, cut])
            grad = part if grad is None else grad + part
        value = grad * gain[:, cut]
        scaled[:, cut] = value
        acc[...] += value * mixed[:, cut]

    @pl.when(step == pl.num_programs(0) - 1)
    def _():
        for i, squares in enumerate((s0, s1, s2)):
            stats[i : i + 1, :] = squares[...]
        stats[SPAN + 1 : SPAN + 2, :] = row_total(acc[...])


def value_grads(blocks, place, keys, queries, cotangents, totals, gain, mixed, squares):
    rows, width = keys.shape
    heads = width // HEAD_DIM
    block = head_block(rows, width)
    stat = whole((heads, rows))
    return per_head(
        functools.partial(value_grads_kernel, blocks),
        place,
        (keys, *queries, *cotangents, *totals, gain, mixed, *squares),
        [block] * 7 + [stat] * 3 + [head_block(1, width), block] + [whole((1, rows))] * 3,
        (jax.ShapeDtypeStruct((rows, width), f32), jax.ShapeDtypeStruct((SPAN + 2, rows), f32)),
        (block, whole((SPAN + 2, rows))),
        scratch=[pltpu.VMEM((rows, LANES), f32)],
        name="value_grads",
        group=width,
        time=7,
    )


def attend_kernel(
    full_width, place, queries, cotangent, k0, k1, k2, v0, v1, v2, stats, totals, attended, grad, delta, columns
):
    position = place[0]

    @pl.when(pl.program_id(0) == 0)
    def _():
        columns[...] = jnp.transpose(totals[...])

    lane = lax.broadcasted_iota(jnp.int32, columns.shape, 1)
    inverses = [inverse_of(stats[i : i + 1, :], full_width) for i in range(SPAN + 1)]
    for head, cut in step_heads(queries):
        log_total = jnp.sum(jnp.where(lane == head, columns[...], 0.0), axis=1, keepdims=True)
        probs = []
        output = None
        for offset, (key, value) in enumerate(((k0, v0), (k1, v1), (k2, v2))):
            scores = rows_by_rows(queries[:, cut], key[:, cut]) * (SCALE * LOG2E)
            scores = masked(scores, offset, position >= offset, False)
            prob = jnp.exp2(scores - log_total)
            probs.append(prob)
            part = product((prob * inverses[offset]).astype(bf16), value[:, cut])
            output = part if output is None else output + part
        result = output.astype(bf16)
        attended[:, cut] = result
        weighed = cotangent[:, cut].astype(f32) * result.astype(f32)
        delta[pl.ds(head, 1), :] = row_total(weighed)
        delta_column = jnp.sum(weighed, axis=1, keepdims=True)
        total = None
        for prob, inverse, key, value in zip(probs, inverses, (k0, k1, k2), (v0, v1, v2)):
            dprob = rows_by_rows(cotangent[:, cut], value[:, cut]) * inverse
            dscore = (prob * (dprob - delta_column)).astype(bf16)
            part = product(dscore, key[:, cut])
            total = part if total is None else total + part
        grad[:, cut] = (total * SCALE).astype(bf16)


def attend(full_width, place, queries, cotangent, keys, values, stats, totals):
    rows, width = queries.shape
    heads = width // HEAD_DIM
    block = head_block(rows)
    stat = whole((heads, rows))
    out = jax.ShapeDtypeStruct((rows, width), bf16)
    return per_head(
        functools.partial(attend_kernel, full_width),
        place,
        (queries, cotangent, *keys, *values, stats, totals),
        [block] * 8 + [whole((SPAN + 2, rows)), stat],
        (out, out, jax.ShapeDtypeStruct((heads, rows), f32)),
        (block, block, stat),
        scratch=[pltpu.VMEM((rows, heads), f32)],
        name="attend",
        vmem=61,
        time=10,
    )


def key_grads_kernel(
    full_width, blocks, place, keys, values, q0, q1, q2, d0, d1, d2, t0, t1, t2, e0, e1, e2, squares, grad
):
    position = place[0]
    inverse = inverse_of(column(squares[0:1, :]), full_width)
    groups = ((q0, d0, t0, e0), (q1, d1, t1, e1), (q2, d2, t2, e2))
    for head, cut in step_heads(keys):
        total = None
        for offset, (query, cotangent, log_total, delta) in enumerate(groups):
            scores = rows_by_rows(keys[:, cut], query[:, cut]) * (SCALE * LOG2E)
            scores = masked(scores, offset, position + offset < blocks, True)
            probs = jnp.exp2(scores - log_total[pl.ds(head, 1), :])
            dprob = rows_by_rows(values[:, cut], cotangent[:, cut]) * inverse
            dscore = (probs * (dprob - delta[pl.ds(head, 1), :])).astype(bf16)
            part = product(dscore, query[:, cut])
            total = part if total is None else total + part
        grad[:, cut] = (total * SCALE).astype(bf16)


def key_grads(full_width, blocks, place, keys, values, queries, cotangents, totals, deltas, squares):
    rows, width = keys.shape
    heads = width // HEAD_DIM
    block = head_block(rows, width)
    stat = whole((heads, rows))
    return per_head(
        functools.partial(key_grads_kernel, full_width, blocks),
        place,
        (keys, values, *queries, *cotangents, *totals, *deltas, squares),
        [block] * 8 + [stat] * 6 + [whole((SPAN + 2, rows))],
        jax.ShapeDtypeStruct((rows, width), bf16),
        block,
        name="key_grads",
        group=width,
        time=8,
    )


def shards(
    mixer_input, gate_in, gate_out, residue, decay_rate, norm_gain, queries, key_vectors, grad_out
):
    length, width = queries.shape
    full_width = width * lax.axis_size("tp")
    blocks = lax.axis_size("ctx")
    place = lax.axis_index("ctx").reshape(1).astype(jnp.int32)
    gain = norm_gain[None, :]
    residue = jnp.transpose(residue)

    keys_1 = shifted(key_vectors, 1)
    keys_2 = shifted(keys_1, 1)
    queries_1 = shifted(queries, -1)
    cotangent_1 = shifted(grad_out, -1)
    queries_2 = shifted(queries_1, -1)
    cotangent_2 = shifted(cotangent_1, -1)

    final, rates = forward_state(mixer_input, gate_in, jnp.transpose(decay_rate))
    carry = carry_in(final, rates, length, False)
    mixed, scaled_mix, squares = forward_mix(
        place, mixer_input, gate_in, rates, residue, carry, gate_out, gain
    )
    mix_1 = shifted(scaled_mix, 1)
    mix_2 = shifted(mix_1, 1)

    totals = row_totals(place, queries, key_vectors, keys_1, keys_2)
    totals_1 = shifted(totals, -1)
    totals_2 = shifted(totals, -2)
    late = after(squares, totals)
    all_squares = (squares, shifted(late, 1), shifted(late, 2))
    all_queries = (queries, queries_1, queries_2)
    all_cotangents = (grad_out, cotangent_1, cotangent_2)
    all_totals = (totals, totals_1, totals_2)
    scaled, stats = value_grads(
        blocks, place, key_vectors, all_queries, all_cotangents, all_totals, gain, mixed, all_squares
    )
    stats = lax.psum(stats, "tp")
    final, drive = backward_state(full_width, scaled, mixed, gate_out, stats, rates)
    carry = carry_in(final, rates, length, True)
    grad_input = backward_mix(place, drive, rates, residue, carry, gate_in)

    attended, grad_queries, delta = attend(
        full_width,
        place,
        queries,
        grad_out,
        (key_vectors, keys_1, keys_2),
        (scaled_mix, mix_1, mix_2),
        stats,
        totals,
    )
    all_deltas = (delta, shifted(delta, -1), shifted(delta, -2))
    grad_keys = key_grads(
        full_width,
        blocks,
        place,
        key_vectors,
        scaled_mix,
        all_queries,
        all_cotangents,
        all_totals,
        all_deltas,
        stats,
    )
    return (attended, grad_queries, grad_keys, grad_input)


def solution(mesh):
    in_specs = (
        P("ctx", "tp"),
        P("ctx", "tp"),
        P("ctx", "tp"),
        P("tp", None),
        P("tp", None),
        P("tp"),
        P("ctx", "tp"),
        P("ctx", "tp"),
        P("ctx", "tp"),
    )
    out_specs = (P("ctx", "tp"), P("ctx", "tp"), P("ctx", "tp"), P("ctx", "tp"))
    return jax.shard_map(shards, mesh=mesh, in_specs=in_specs, out_specs=out_specs, check_vma=False)
```
